256 devices in a mesh: expert: 16 (over z_hi, y, core), space: 16 (over x, z_lo).
Axes of the slice: x: 4, y: 4, z: 8 (z_hi: 2, z_lo: 4; z = z_hi * 4 + z_lo), core: 2. Of those that a mesh axis runs over, the one named last changes fastest.
Arguments:
- attn_inputs: bfloat16 [3, 16, 192, 12, 512], P(None, 'expert', 'space'), may hold values from -9 to 9
- residual: bfloat16 [16, 192, 12, 512], P('expert', 'space'), may hold values from -400 to 400
- logits: float32 [16, 192, 12, 32], P('expert', 'space'), may hold values from -12 to 454
- expert_ids: int32 [16, 192, 12, 2], P('expert', 'space'), may hold values from 0 to 31, all different within a row; in each aligned block of 144 rows (0 to 143, 144 to 287, ..., all dimensions but the last counted through in order) at most 12 rows name the same one
- keep_mask: int32 [16, 192, 12, 2], P('expert', 'space'), may hold values 0 or 1
- cotangent: bfloat16 [16, 192, 12, 512], P('expert', 'space'), may hold values from -1.5 to 1.5
- up_weight: bfloat16 [32, 512, 2048], P('expert', None, 'space'), may hold values from -0.25 to 0.25
- down_weight: bfloat16 [32, 512, 2048], P('expert', None, 'space'), may hold values from -0.125 to 0.125
Outputs:
- attn_grad: bfloat16 [3, 16, 192, 12, 512], P(None, 'expert', 'space')
- residual_grad: bfloat16 [16, 192, 12, 512], P('expert', 'space')
- up_grad: float32 [32, 512, 2048], P('expert', None, 'space')
- down_grad: float32 [32, 512, 2048], P('expert', None, 'space')
- logit_grad: float32 [16, 192, 12, 32], P('expert', 'space')
The draws below stay inside these ranges and needn't reach their ends.
Inputs may be any that keep to these rules, and one draw needn't show every extreme that they name: `expert_ids`: each token names 2 different experts; among the tokens of one strip no expert is named more than 12 times, and in every draw some expert is named exactly 12 times by the tokens of some strip.
All inputs are finite; a program needn't handle non-finite values. No bound on the sum of `keep_mask` on one device may be relied on, other than what follows from the above.
Results may differ from the reference program's by a relative error of at most 0.012.
Values may be sent and summed in bfloat16 or wider, within the bound.
A program may use at most 128 MiB of HBM per device.

```python
import math
import jax
import jax.numpy as jnp
import numpy as np
from jax import lax

C = 512
HEADS = 16
F = 2048
EXPERTS = 32
WIN = 12
TOP = 2
WW = 12
SHIFT = 6
NIMG = 16
IMG_H = 192
TOK_DEV = 144
CAP = 12
N_SPACE = 16


def draw_attn_inputs(key, part):
    full_shape = (3, NIMG, IMG_H, WW, C)
    key_base = jax.random.fold_in(key, 0)
    base_draw = jnp.clip(jax.random.normal(key_base, full_shape, jnp.float32), -4.0, 4.0)
    return base_draw.astype(jnp.bfloat16)


def draw_residual(key, part):
    full_shape = (NIMG, IMG_H, WW, C)
    key_base, key_rows, key_cols = jax.random.split(key, 3)
    base_draw = jnp.clip(jax.random.normal(key_base, full_shape, jnp.float32), -4.0, 4.0)
    row_scale = jnp.exp(jax.random.uniform(key_rows, (NIMG, IMG_H, WW, 1), jnp.float32, 0.0, math.log(10.0)))
    col_scale = jnp.exp(jax.random.uniform(key_cols, (C,), jnp.float32, 0.0, math.log(10.0)))
    return (base_draw * row_scale * col_scale).astype(jnp.bfloat16)


def draw_logits(key, part):
    full_shape = (NIMG, IMG_H, WW, EXPERTS)
    key_base = jax.random.fold_in(key, 0)
    base_draw = jnp.clip(3.0 * jax.random.normal(key_base, full_shape, jnp.float32), -12.0, 12.0)
    return base_draw


def set_ends(entries, rng, smallest, largest):
    longest = entries.shape.index(max(entries.shape))
    spots = []
    for shift in (0, 1):
        where = [jax.random.randint(jax.random.fold_in(rng, axis), (), 0, length) for axis, length in enumerate(entries.shape)]
        where[longest] = (where[longest] + shift) % entries.shape[longest]
        spots.append(tuple(where))
    return entries.at[spots[0]].set(smallest).at[spots[1]].set(largest)


def steps_of(own_key, extent, pieces, smallest, top_value):
    factor_of = 1.0
    for axis_at, shards_of in pieces:
        heights = jax.random.uniform(jax.random.fold_in(jax.random.fold_in(own_key, 6), axis_at), (shards_of,), jnp.float32, smallest / len(pieces), top_value / len(pieces))
        factor_of = factor_of * jnp.repeat(jnp.exp(heights), extent[axis_at] // shards_of).reshape((-1,) + (1,) * (len(extent) - 1 - axis_at))
    return factor_of


def assign_block(stream_key, own, number, rows, count, top, limit, lean):
    sequence = jax.random.permutation(stream_key, count)
    packed, common = load_shares(count, rows * top, limit, lean, True), load_shares(count, rows * top, limit, lean, False)
    places = jnp.arange(count)

    def named(sizes, offset_by):
        used = int((sizes > 0).sum())
        fixed = max(1, used // 4)
        shifted = fixed + (places - fixed + offset_by * (used - fixed)) % max(1, count - fixed)
        return jnp.zeros((count,), jnp.int32).at[sequence[jnp.where(places < fixed, places, shifted)]].set(jnp.asarray(sizes, jnp.int32))

    sizes = jnp.where(number % 4 == 0, named(packed, number // 4), named(common, number - number // 4 - 1))
    mixed = jax.random.permutation(jax.random.fold_in(own, 3), count)
    giver, receiver = mixed[0:count // 2 * 2:2], mixed[1:count // 2 * 2:2]
    margin = jnp.minimum(sizes[giver] - 1, limit - sizes[receiver]) // 2
    margin = jnp.where((giver == sequence[0]) | (receiver == sequence[0]) | (sizes[receiver] == 0), 0, jnp.maximum(margin, 0))
    shifted = jax.random.randint(jax.random.fold_in(own, 4), (count // 2,), 0, 1 << 20) % (margin + 1)
    sizes = sizes.at[giver].add(-shifted).at[receiver].add(shifted)
    labels = jnp.searchsorted(jnp.cumsum(sizes), jnp.arange(rows * top), side="right").astype(jnp.int32)
    table = labels.reshape(top, rows).T
    table = table[jax.random.permutation(jax.random.fold_in(own, 1), rows)]
    offset_by = jax.random.randint(jax.random.fold_in(own, 2), (rows, 1), 0, top)
    return jnp.take_along_axis(table, (jnp.arange(top)[None, :] + offset_by) % top, axis=1)


def load_shares(count, total, most, lean, full):
    weights = [(1 << 20) // math.isqrt(rank ** lean) + 1 for rank in range(1, count + 1)]
    largest = most if full else min(most, max(-(-total // count), total * weights[0] // sum(weights)))
    least = 1 if total - largest >= count - 1 else 0
    holding, spare = [largest] + [least] * (count - 1), total - largest - least * (count - 1)
    while spare > 0:
        movable = [i for i in range(1, count) if holding[i] < largest] or [i for i in range(1, count) if holding[i] < most]
        whole, remaining = sum([weights[i] for i in movable]), spare
        for i in movable:
            addition = min(most - holding[i], max(1, remaining * weights[i] // whole), spare)
            holding[i] = holding[i] + addition
            spare = spare - addition
    return np.array(holding)


def centred(key, dims, deviation, most, cuts=(), held_as=jnp.bfloat16):
    result = deviation * jax.random.normal(key, dims, jnp.float32)
    if cuts:
        result = result * steps_of(key, dims, cuts, -0.22, 0.18)
    return jnp.clip(result, -most, most).astype(held_as)


def setup_inputs(seed: int = 0) -> dict:
    key_of = jax.random.split(jax.random.key(seed), 9)
    attn_inputs = draw_attn_inputs(jax.random.fold_in(key_of[8], 71), 0)
    residual = draw_residual(jax.random.fold_in(key_of[8], 71), 0)
    logits = draw_logits(jax.random.fold_in(key_of[8], 71), 0)
    expert_ids_keys = jax.random.split(jax.random.fold_in(key_of[3], 1), NIMG * IMG_H * WW // TOK_DEV)
    expert_ids_turns = jax.random.permutation(jax.random.fold_in(key_of[3], 3), NIMG * IMG_H * WW // TOK_DEV)
    expert_ids = jax.vmap(lambda own, number: assign_block(jax.random.fold_in(key_of[3], 2), own, number, TOK_DEV, EXPERTS, TOP, CAP, 1))(expert_ids_keys, expert_ids_turns).reshape((NIMG, IMG_H, WW, TOP))
    keep_mask = set_ends((jax.random.randint(key_of[4], (NIMG, IMG_H, WW, TOP), 0, 16) < 15).astype(jnp.int32), jax.random.fold_in(key_of[4], 1), 0, 1)
    cotangent = centred(key_of[5], (NIMG, IMG_H, WW, C), 0.25, 1.5, ((0, 16), (1, 16)))
    up_weight = centred(key_of[6], (EXPERTS, C, F), C ** -0.5, 0.25, ((0, 16), (2, 16)))
    down_weight = centred(key_of[7], (EXPERTS, C, F), F ** -0.5, 0.125, ((0, 16), (2, 16)))
    return dict(attn_inputs=attn_inputs, residual=residual, logits=logits, expert_ids=expert_ids, keep_mask=keep_mask, cotangent=cotangent, up_weight=up_weight, down_weight=down_weight)


NORM_EPS = 1e-06
SCORE_MASK = -100.0

def gelu_pair(pre_act):
    activation, pullback = jax.vjp(jax.nn.gelu, pre_act)
    gelu_slope = pullback(jnp.ones_like(pre_act))[0]
    return (activation, gelu_slope)

def to_windows(tensor, head_count):
    blocks, win_side, map_width, channels = tensor.shape
    win_count = map_width // win_side
    head_dim = channels // head_count
    shaped = tensor.reshape(blocks, win_side, win_count, win_side, head_count, head_dim)
    shaped = shaped.transpose(0, 2, 4, 1, 3, 5)
    return shaped.reshape(blocks, win_count, head_count, win_side * win_side, head_dim)

def from_windows(tensor, win_side):
    blocks, win_count, head_count, win_area, head_dim = tensor.shape
    shaped = tensor.reshape(blocks, win_count, head_count, win_side, win_side, head_dim)
    shaped = shaped.transpose(0, 3, 1, 4, 2, 5)
    return shaped.reshape(blocks, win_side, win_count * win_side, head_count * head_dim)

def window_grads(frame_qkv, frame_grad, last_flags, head_count):
    win_side = frame_grad.shape[1]
    map_width = frame_grad.shape[2]
    half_win = win_side // 2
    head_dim = frame_grad.shape[3] // head_count
    inv_sqrt = head_dim ** (-0.5)
    highest = lax.Precision.HIGHEST
    rolled = jnp.roll(frame_qkv, -half_win, axis=3)
    grad_rolled = jnp.roll(frame_grad, -half_win, axis=2)
    query_win = to_windows(rolled[0], head_count).astype(jnp.float32)
    key_win = to_windows(rolled[1], head_count).astype(jnp.float32)
    value_win = to_windows(rolled[2], head_count).astype(jnp.float32)
    grad_win = to_windows(grad_rolled, head_count).astype(jnp.float32)
    row_pos = jnp.arange(win_side, dtype=jnp.int32)
    col_pos = jnp.arange(map_width, dtype=jnp.int32)
    row_label = jnp.where(last_flags[:, None], jnp.where(row_pos < half_win, 1, 2)[None, :], 0)
    col_label = jnp.where(col_pos >= map_width - win_side, jnp.where(col_pos < map_width - half_win, 1, 2), 0)
    region = 3 * row_label[:, :, None] + col_label[None, None, :]
    region = region.reshape(region.shape[0], win_side, map_width // win_side, win_side).transpose(0, 2, 1, 3)
    region = region.reshape(region.shape[0], region.shape[1], win_side * win_side)
    score_bias = jnp.where(region[:, :, :, None] != region[:, :, None, :], SCORE_MASK, 0.0)[:, :, None]
    scores = jnp.einsum('bnhqd,bnhkd->bnhqk', query_win, key_win, precision=highest) * inv_sqrt + score_bias
    row_max = lax.optimization_barrier(jnp.max(scores, axis=-1, keepdims=True))
    exp_scores = jnp.exp(scores - row_max)
    attn_probs = exp_scores / lax.optimization_barrier(jnp.sum(exp_scores, axis=-1, keepdims=True))
    weights_bf = attn_probs.astype(jnp.bfloat16).astype(jnp.float32)
    attn_out = jnp.einsum('bnhqk,bnhkd->bnhqd', weights_bf, value_win, precision=highest)
    row_delta = lax.optimization_barrier(jnp.sum(grad_win * attn_out, axis=-1, keepdims=True))
    prob_grad = jnp.einsum('bnhqd,bnhkd->bnhqk', grad_win, value_win, precision=highest)
    score_grad = (attn_probs * (prob_grad - row_delta)).astype(jnp.bfloat16).astype(jnp.float32)
    query_grad = (jnp.einsum('bnhqk,bnhkd->bnhqd', score_grad, key_win, precision=highest) * inv_sqrt).astype(jnp.bfloat16)
    key_grad = (jnp.einsum('bnhqk,bnhqd->bnhkd', score_grad, query_win, precision=highest) * inv_sqrt).astype(jnp.bfloat16)
    value_grad = jnp.einsum('bnhqk,bnhqd->bnhkd', weights_bf, grad_win, precision=highest).astype(jnp.bfloat16)
    stacked = jnp.stack([from_windows(query_grad, win_side), from_windows(key_grad, win_side), from_windows(value_grad, win_side)])
    return jnp.roll(stacked, half_win, axis=3)

def expert_pass(operands):
    in_rows, cot_rows, scaled, up_mat, down_mat = operands
    pre_act = jnp.dot(in_rows, up_mat, preferred_element_type=jnp.float32)
    activation, gelu_slope = gelu_pair(pre_act)
    act_bf = activation.astype(jnp.bfloat16)
    expert_out = jnp.dot(act_bf, down_mat.T, preferred_element_type=jnp.float32)
    row_dots = lax.optimization_barrier(jnp.sum(cot_rows.astype(jnp.float32) * expert_out, axis=-1)).astype(jnp.bfloat16)
    pre_grad = (jnp.dot(scaled, down_mat, preferred_element_type=jnp.float32) * gelu_slope).astype(jnp.bfloat16)
    row_grad = jnp.dot(pre_grad, up_mat.T, preferred_element_type=jnp.float32).astype(jnp.bfloat16)
    up_part = jnp.dot(in_rows.T, pre_grad, preferred_element_type=jnp.float32)
    down_part = jnp.dot(scaled.T, act_bf, preferred_element_type=jnp.float32)
    return (row_grad, row_dots, up_part, down_part)

def reference(attn_inputs, residual, logits, expert_ids, keep_mask, cotangent, up_weight, down_weight):
    groups_total = NIMG * N_SPACE
    resid_float = residual.reshape(groups_total, TOK_DEV, C).astype(jnp.float32)
    rms_value = jnp.sqrt(lax.optimization_barrier(jnp.mean(resid_float * resid_float, axis=-1, keepdims=True)) + NORM_EPS)
    norm_float = resid_float / rms_value
    normed = norm_float.astype(jnp.bfloat16)
    route_ids = expert_ids.reshape(groups_total, TOK_DEV, TOP)
    keep_float = keep_mask.reshape(groups_total, TOK_DEV, TOP).astype(jnp.float32)
    router_logits = logits.reshape(groups_total, TOK_DEV, EXPERTS)
    expert_cols = jnp.arange(EXPERTS, dtype=jnp.int32)
    one_hot = route_ids[..., None] == expert_cols
    chosen = lax.optimization_barrier(jnp.sum(jnp.where(one_hot, router_logits[:, :, None, :], 0.0), axis=-1))
    chosen_max = lax.optimization_barrier(jnp.max(chosen, axis=-1, keepdims=True))
    chosen_exp = jnp.exp(chosen - chosen_max)
    gates_top = chosen_exp / lax.optimization_barrier(jnp.sum(chosen_exp, axis=-1, keepdims=True))
    gate_weight = gates_top * keep_float
    cot_rows = cotangent.reshape(groups_total, TOK_DEV, C)
    scaled_rows = (gate_weight[..., None] * cot_rows[:, :, None, :].astype(jnp.float32)).astype(jnp.bfloat16)
    flat_hot = one_hot.reshape(groups_total, TOK_DEV * TOP, EXPERTS).astype(jnp.int32)
    running = (jnp.cumsum(flat_hot, axis=1) - flat_hot).astype(jnp.int32)
    slot_index = lax.optimization_barrier(jnp.sum(running * flat_hot, axis=-1)).astype(jnp.int32)
    flat_ids = route_ids.reshape(groups_total, TOK_DEV * TOP).astype(jnp.int32)
    group_index = jnp.arange(groups_total, dtype=jnp.int32)[:, None]
    destination = ((flat_ids * groups_total + group_index) * CAP + slot_index).reshape(-1).astype(jnp.int32)
    slot_total = EXPERTS * groups_total * CAP
    expert_rows = groups_total * CAP
    choice_norm = jnp.broadcast_to(normed[:, :, None, :], (groups_total, TOK_DEV, TOP, C)).reshape(-1, C)
    choice_cot = jnp.broadcast_to(cot_rows[:, :, None, :], (groups_total, TOK_DEV, TOP, C)).reshape(-1, C)
    norm_buffer = jnp.zeros((slot_total, C), jnp.bfloat16).at[destination].set(choice_norm)
    cot_buffer = jnp.zeros((slot_total, C), jnp.bfloat16).at[destination].set(choice_cot)
    scaled_buffer = jnp.zeros((slot_total, C), jnp.bfloat16).at[destination].set(scaled_rows.reshape(-1, C))
    row_grad, row_dots, up_grad, down_grad = lax.map(expert_pass, (norm_buffer.reshape(EXPERTS, expert_rows, C), cot_buffer.reshape(EXPERTS, expert_rows, C), scaled_buffer.reshape(EXPERTS, expert_rows, C), up_weight, down_weight))
    choice_grad = row_grad.reshape(slot_total, C)[destination].astype(jnp.float32).reshape(groups_total, TOK_DEV, TOP, C)
    norm_grad = lax.optimization_barrier(jnp.sum(choice_grad, axis=2))
    inner_mean = lax.optimization_barrier(jnp.mean(norm_grad * norm_float, axis=-1, keepdims=True))
    residual_grad = (cot_rows.astype(jnp.float32) + (norm_grad - norm_float * inner_mean) / rms_value).astype(jnp.bfloat16)
    choice_dots = row_dots.reshape(slot_total)[destination].astype(jnp.float32).reshape(groups_total, TOK_DEV, TOP)
    gate_drive = keep_float * choice_dots
    gate_mix = lax.optimization_barrier(jnp.sum(gates_top * gate_drive, axis=-1, keepdims=True))
    gate_part = gates_top * (gate_drive - gate_mix)
    logit_gate = lax.optimization_barrier(jnp.sum(jnp.where(one_hot, gate_part[..., None], 0.0), axis=2))
    expert_share = lax.optimization_barrier(jnp.sum(jnp.where(one_hot, keep_float[..., None], 0.0), axis=(1, 2))) / (TOP * TOK_DEV)
    logit_max = lax.optimization_barrier(jnp.max(router_logits, axis=-1, keepdims=True))
    logit_exp = jnp.exp(router_logits - logit_max)
    router_probs = logit_exp / lax.optimization_barrier(jnp.sum(logit_exp, axis=-1, keepdims=True))
    share_mean = lax.optimization_barrier(jnp.sum(router_probs * expert_share[:, None, :], axis=-1, keepdims=True))
    balance = EXPERTS * router_probs * (expert_share[:, None, :] - share_mean)
    logit_grad = (logit_gate + balance).reshape(NIMG, IMG_H, WW, EXPERTS)
    residual_map = residual_grad.reshape(NIMG, IMG_H, WW, C)
    last_flags = jnp.arange(N_SPACE, dtype=jnp.int32) == N_SPACE - 1

    def image_pass(operands):
        image_qkv, image_grad = operands
        frame_qkv = jnp.roll(image_qkv, -SHIFT, axis=1).reshape(3, N_SPACE, WIN, WW, C)
        frame_grad = jnp.roll(image_grad, -SHIFT, axis=0).reshape(N_SPACE, WIN, WW, C)
        frame_grads = window_grads(frame_qkv, frame_grad, last_flags, HEADS)
        return jnp.roll(frame_grads.reshape(3, IMG_H, WW, C), SHIFT, axis=1)
    image_grads = lax.map(image_pass, (jnp.moveaxis(attn_inputs, 1, 0), residual_map))
    attn_grad = jnp.moveaxis(image_grads, 0, 1)
    return (attn_grad, residual_map, up_grad, down_grad, logit_grad)
```

```python
import jax
import jax.numpy as jnp
from jax import lax
from jax.sharding import PartitionSpec as P

HEADS = 16
EXPERTS = 32
TOP = 2
CAP = 12


NORM_EPS = 1e-06
SCORE_MASK = -100.0


def from_behind(block, axis, distance):
    devices = range(lax.axis_size(axis))
    route = [((i - distance) % len(devices), i) for i in devices]
    return lax.ppermute(block, axis, route)


def gelu_pair(pre_act):
    activation, pullback = jax.vjp(jax.nn.gelu, pre_act)
    gelu_slope = pullback(jnp.ones_like(pre_act))[0]
    return (activation, gelu_slope)


def to_windows(tensor, head_count):
    blocks, win_side, map_width, channels = tensor.shape
    win_count = map_width // win_side
    head_dim = channels // head_count
    shaped = tensor.reshape(blocks, win_side, win_count, win_side, head_count, head_dim)
    shaped = shaped.transpose(0, 2, 4, 1, 3, 5)
    return shaped.reshape(blocks, win_count, head_count, win_side * win_side, head_dim)


def from_windows(tensor, win_side):
    blocks, win_count, head_count, win_area, head_dim = tensor.shape
    shaped = tensor.reshape(blocks, win_count, head_count, win_side, win_side, head_dim)
    shaped = shaped.transpose(0, 3, 1, 4, 2, 5)
    return shaped.reshape(blocks, win_side, win_count * win_side, head_count * head_dim)


def window_grads(frame_qkv, frame_grad, last_flags, head_count):
    win_side = frame_grad.shape[1]
    map_width = frame_grad.shape[2]
    half_win = win_side // 2
    head_dim = frame_grad.shape[3] // head_count
    inv_sqrt = head_dim ** (-0.5)
    rolled = jnp.roll(frame_qkv, -half_win, axis=3)
    grad_rolled = jnp.roll(frame_grad, -half_win, axis=2)
    query_win = to_windows(rolled[0], head_count)
    key_win = to_windows(rolled[1], head_count)
    value_win = to_windows(rolled[2], head_count)
    grad_win = to_windows(grad_rolled, head_count)
    row_pos = jnp.arange(win_side, dtype=jnp.int32)
    col_pos = jnp.arange(map_width, dtype=jnp.int32)
    row_label = jnp.where(last_flags[:, None], jnp.where(row_pos < half_win, 1, 2)[None, :], 0)
    col_label = jnp.where(
        col_pos >= map_width - win_side, jnp.where(col_pos < map_width - half_win, 1, 2), 0
    )
    region = 3 * row_label[:, :, None] + col_label[None, None, :]
    region = region.reshape(region.shape[0], win_side, map_width // win_side, win_side).transpose(
        0, 2, 1, 3
    )
    region = region.reshape(region.shape[0], region.shape[1], win_side * win_side)
    score_bias = jnp.where(region[:, :, :, None] != region[:, :, None, :], SCORE_MASK, 0.0)[
        :, :, None
    ]
    scores = (
        jnp.einsum("bnhqd,bnhkd->bnhqk", query_win, key_win, preferred_element_type=jnp.float32)
        * inv_sqrt
        + score_bias
    )
    row_max = jnp.max(scores, axis=-1, keepdims=True)
    exp_scores = jnp.exp(scores - row_max)
    attn_probs = exp_scores / jnp.sum(exp_scores, axis=-1, keepdims=True)
    weights_bf = attn_probs.astype(jnp.bfloat16)
    attn_out = jnp.einsum(
        "bnhqk,bnhkd->bnhqd", weights_bf, value_win, preferred_element_type=jnp.float32
    )
    row_delta = jnp.sum(grad_win.astype(jnp.float32) * attn_out, axis=-1, keepdims=True)
    prob_grad = jnp.einsum(
        "bnhqd,bnhkd->bnhqk", grad_win, value_win, preferred_element_type=jnp.float32
    )
    score_grad = (attn_probs * (prob_grad - row_delta)).astype(jnp.bfloat16)
    query_grad = (
        jnp.einsum("bnhqk,bnhkd->bnhqd", score_grad, key_win, preferred_element_type=jnp.float32)
        * inv_sqrt
    ).astype(jnp.bfloat16)
    key_grad = (
        jnp.einsum("bnhqk,bnhqd->bnhkd", score_grad, query_win, preferred_element_type=jnp.float32)
        * inv_sqrt
    ).astype(jnp.bfloat16)
    value_grad = jnp.einsum(
        "bnhqk,bnhqd->bnhkd", weights_bf, grad_win, preferred_element_type=jnp.float32
    ).astype(jnp.bfloat16)
    stacked = jnp.stack(
        [
            from_windows(query_grad, win_side),
            from_windows(key_grad, win_side),
            from_windows(value_grad, win_side),
        ]
    )
    return jnp.roll(stacked, half_win, axis=3)


def per_device(
    attn_inputs, residual, logits, expert_ids, keep_mask, cotangent, up_weight, down_weight
):
    group_count = lax.axis_size("expert")
    local_experts = up_weight.shape[0]
    win_side = residual.shape[1]
    map_width = residual.shape[2]
    channels = residual.shape[3]
    tokens = win_side * map_width
    half_win = win_side // 2
    space_index = lax.axis_index("space")
    space_count = lax.axis_size("space")
    qkv_local = attn_inputs[:, 0]
    next_rows = from_behind(qkv_local[:, :half_win], "space", -1)
    qkv_shifted = jnp.concatenate([qkv_local[:, half_win:], next_rows], axis=1)
    resid_float = residual[0].reshape(tokens, channels).astype(jnp.float32)
    rms_value = jnp.sqrt(jnp.mean(resid_float * resid_float, axis=-1, keepdims=True) + NORM_EPS)
    norm_float = resid_float / rms_value
    normed = norm_float.astype(jnp.bfloat16)
    route_ids = expert_ids[0].reshape(tokens, TOP)
    keep_float = keep_mask[0].reshape(tokens, TOP).astype(jnp.float32)
    router_logits = logits[0].reshape(tokens, EXPERTS)
    expert_cols = jnp.arange(EXPERTS, dtype=jnp.int32)
    one_hot = route_ids[:, :, None] == expert_cols[None, None, :]
    chosen = jnp.sum(jnp.where(one_hot, router_logits[:, None, :], 0.0), axis=-1)
    chosen_max = jnp.max(chosen, axis=-1, keepdims=True)
    chosen_exp = jnp.exp(chosen - chosen_max)
    gates_top = chosen_exp / jnp.sum(chosen_exp, axis=-1, keepdims=True)
    gate_weight = gates_top * keep_float
    cot_rows = cotangent[0].reshape(tokens, channels)
    scaled_rows = (gate_weight[:, :, None] * cot_rows[:, None, :].astype(jnp.float32)).astype(
        jnp.bfloat16
    )
    flat_hot = one_hot.reshape(tokens * TOP, EXPERTS).astype(jnp.float32)
    choice_pos = jnp.arange(tokens * TOP, dtype=jnp.int32)
    earlier = (choice_pos[None, :] < choice_pos[:, None]).astype(jnp.bfloat16)
    running = jnp.dot(earlier, flat_hot.astype(jnp.bfloat16), preferred_element_type=jnp.float32)
    slot_index = jnp.sum(running * flat_hot, axis=-1).astype(jnp.int32)
    flat_ids = route_ids.reshape(-1)
    destination = (
        flat_ids % local_experts * group_count + flat_ids // local_experts
    ) * CAP + slot_index
    slot_total = local_experts * group_count * CAP
    choice_norm = jnp.broadcast_to(normed[:, None, :], (tokens, TOP, channels)).reshape(
        tokens * TOP, channels
    )
    choice_cot = jnp.broadcast_to(cot_rows[:, None, :], (tokens, TOP, channels)).reshape(
        tokens * TOP, channels
    )
    send_norm = (
        jnp.zeros((slot_total, channels), jnp.bfloat16)
        .at[destination]
        .set(choice_norm)
        .reshape(local_experts, group_count, CAP, channels)
    )
    send_cot = (
        jnp.zeros((slot_total, channels), jnp.bfloat16)
        .at[destination]
        .set(choice_cot)
        .reshape(local_experts, group_count, CAP, channels)
    )
    send_scaled = (
        jnp.zeros((slot_total, channels), jnp.bfloat16)
        .at[destination]
        .set(scaled_rows.reshape(tokens * TOP, channels))
        .reshape(local_experts, group_count, CAP, channels)
    )
    recv_norm, recv_cot, recv_scaled = (
        lax.all_to_all(send_norm, "expert", split_axis=1, concat_axis=1, tiled=True),
        lax.all_to_all(send_cot, "expert", split_axis=1, concat_axis=1, tiled=True),
        lax.all_to_all(send_scaled, "expert", split_axis=1, concat_axis=1, tiled=True),
    )
    expert_rows = group_count * CAP
    in_rows = recv_norm.reshape(local_experts, expert_rows, channels)
    cot_in = recv_cot.reshape(local_experts, expert_rows, channels)
    scaled = recv_scaled.reshape(local_experts, expert_rows, channels)
    up_piece = lax.all_gather(up_weight, "space", axis=2, tiled=True)
    down_piece = lax.all_gather(down_weight, "space", axis=2, tiled=True)
    pre_act = jnp.einsum("erc,ecf->erf", in_rows, up_piece, preferred_element_type=jnp.float32)
    activation, gelu_slope = gelu_pair(pre_act)
    act_bf = activation.astype(jnp.bfloat16)
    out_sum = jnp.einsum("erf,ecf->erc", act_bf, down_piece, preferred_element_type=jnp.float32)
    pre_grad = (
        jnp.einsum("erc,ecf->erf", scaled, down_piece, preferred_element_type=jnp.float32)
        * gelu_slope
    ).astype(jnp.bfloat16)
    grad_sum = jnp.einsum("erf,ecf->erc", pre_grad, up_piece, preferred_element_type=jnp.float32)
    up_term = jnp.einsum("erc,erf->ecf", in_rows, pre_grad, preferred_element_type=jnp.float32)
    down_term = jnp.einsum("erc,erf->ecf", scaled, act_bf, preferred_element_type=jnp.float32)
    first_store = up_term
    second_store = down_term
    out_sum, grad_sum, first_store, second_store = (out_sum, grad_sum, first_store, second_store)
    row_dots = jnp.sum(cot_in.astype(jnp.float32) * out_sum, axis=-1).astype(jnp.bfloat16)
    back_grad = grad_sum.astype(jnp.bfloat16).reshape(local_experts, group_count, CAP, channels)
    ret_grad, ret_dots = (
        lax.all_to_all(back_grad, "expert", split_axis=1, concat_axis=1, tiled=True),
        lax.all_to_all(
            row_dots.reshape(local_experts, group_count, CAP),
            "expert",
            split_axis=1,
            concat_axis=1,
            tiled=True,
        ),
    )
    up_grad, down_grad = (
        lax.psum_scatter(first_store, "space", scatter_dimension=2, tiled=True),
        lax.psum_scatter(second_store, "space", scatter_dimension=2, tiled=True),
    )
    choice_grad = (
        ret_grad.reshape(slot_total, channels)[destination]
        .astype(jnp.float32)
        .reshape(tokens, TOP, channels)
    )
    norm_grad = jnp.sum(choice_grad, axis=1)
    inner_mean = jnp.mean(norm_grad * norm_float, axis=-1, keepdims=True)
    residual_grad = (
        cot_rows.astype(jnp.float32) + (norm_grad - norm_float * inner_mean) / rms_value
    ).astype(jnp.bfloat16)
    choice_dots = ret_dots.reshape(slot_total)[destination].astype(jnp.float32).reshape(tokens, TOP)
    gate_drive = keep_float * choice_dots
    gate_mix = jnp.sum(gates_top * gate_drive, axis=-1, keepdims=True)
    gate_part = gates_top * (gate_drive - gate_mix)
    logit_gate = jnp.sum(jnp.where(one_hot, gate_part[:, :, None], 0.0), axis=1)
    expert_share = jnp.sum(jnp.where(one_hot, keep_float[:, :, None], 0.0), axis=(0, 1)) / (
        TOP * tokens
    )
    logit_max = jnp.max(router_logits, axis=-1, keepdims=True)
    logit_exp = jnp.exp(router_logits - logit_max)
    router_probs = logit_exp / jnp.sum(logit_exp, axis=-1, keepdims=True)
    share_mean = jnp.sum(router_probs * expert_share[None, :], axis=-1, keepdims=True)
    balance = EXPERTS * router_probs * (expert_share[None, :] - share_mean)
    logit_grad = (logit_gate + balance).reshape(1, win_side, map_width, EXPERTS)
    grad_map = residual_grad.reshape(win_side, map_width, channels)
    next_grad = from_behind(grad_map[:half_win], "space", -1)
    grad_shifted = jnp.concatenate([grad_map[half_win:], next_grad], axis=0)
    last_flags = jnp.reshape(space_index == space_count - 1, (1,))
    frame_grads = window_grads(qkv_shifted[:, None], grad_shifted[None], last_flags, HEADS)[:, 0]
    prev_rows = from_behind(frame_grads[:, half_win:], "space", 1)
    attn_grad = jnp.concatenate([prev_rows, frame_grads[:, :half_win]], axis=1)
    return (attn_grad[:, None], grad_map[None], up_grad, down_grad, logit_grad)


def solution(mesh):
    in_specs = (
        P(None, "expert", "space", None, None),
        P("expert", "space", None, None),
        P("expert", "space", None, None),
        P("expert", "space", None, None),
        P("expert", "space", None, None),
        P("expert", "space", None, None),
        P("expert", None, "space"),
        P("expert", None, "space"),
    )
    out_specs = (
        P(None, "expert", "space", None, None),
        P("expert", "space", None, None),
        P("expert", None, "space"),
        P("expert", None, "space"),
        P("expert", "space", None, None),
    )
    return jax.shard_map(
        per_device, mesh=mesh, in_specs=in_specs, out_specs=out_specs, check_vma=False
    )
```

```python
import jax
import jax.numpy as jnp
from jax import lax
from jax.experimental import pallas as pl
from jax.experimental.pallas import tpu as pltpu
from jax.sharding import PartitionSpec as P

WIN = 12
PADW = 16
TOK = WIN * PADW
HALF = TOK // 2
C = 512
HEADS = 16
EXPERTS = 32
CAP = 12
NE = 16
NX = 4
NZ = 4
HID = 128
NORM_EPS = 1e-06
SCORE_MASK = -100.0
NO_KEY = -1e30
GELU_C = 0.7978845608028654
GELU_A = 0.044715
F32 = jnp.float32
BF16 = jnp.bfloat16
I32 = jnp.int32


def iota(shape, dim):
    return lax.broadcasted_iota(I32, shape, dim)


def dot(a, b):
    return lax.dot_general(a, b, (((1,), (0,)), ((), ())), preferred_element_type=F32)


def dot_nt(a, b):
    return lax.dot_general(a, b, (((1,), (1,)), ((), ())), preferred_element_type=F32)


def dot_tn(a, b):
    return lax.dot_general(a, b, (((0,), (0,)), ((), ())), preferred_element_type=F32)


def ge(a, n):
    return (a >= n).astype(I32)


def ones_where(cond):
    return jnp.where(cond, 1.0, 0.0).astype(BF16)


def split_tail(x):
    total = x[96:97] + x[97:98]
    high = total.astype(BF16).astype(F32)
    low = total - high
    row = iota((16, C), 0)
    tail = jnp.where(row == 0, high, jnp.where(row == 1, low, 0.0))
    return jnp.concatenate([x[:96], tail], axis=0).astype(BF16)


def kernel(
    attn_ref, resid_ref, logit_ref, ids_ref, keep_ref, cot_ref, up_ref, down_ref,
    attn_out, res_out, up_out, down_out, logit_out,
    qw, qsend, gw, gsend, agrad, asend, arecv,
    resid_s, cot_s, lg_s, ids_s, keep_s, cols, stage, probs, perm_s, bias_s,
    send_rows, recv_rows, rows_all, w_all, wcat, pg_s, act_s, part, xs, xr,
    ret_send, ret_recv, grads, zsend, zrecv,
    d_ss, d_rs, g_ss, g_rs, w_ss, w_rs, x_ss, x_rs, r_ss, r_rs, z_ss, z_rs, h_ss, h_rs,
):
    me_e = lax.axis_index("expert")
    me_s = lax.axis_index("space")
    mx = me_s // NZ
    mz = me_s % NZ
    zhi = me_e // 8
    x1 = mx + 1 - 2 * (mx % 2)
    x3 = NX - 1 - mx
    x2 = NX - 1 - x1
    z1 = mz + 1 - 2 * (mz % 2)
    z3 = NZ - 1 - mz
    z2 = NZ - 1 - z1
    dev_x1 = x1 * NZ + mz
    dev_x3 = x3 * NZ + mz
    dev_z1 = mx * NZ + z1
    dev_z2 = mx * NZ + z2
    after = (me_s + 1) % (NX * NZ)
    before = (me_s + NX * NZ - 1) % (NX * NZ)

    def remote(src, dst, ss, rs, e, s):
        return pltpu.make_async_remote_copy(
            src_ref=src, dst_ref=dst, send_sem=ss, recv_sem=rs,
            device_id={"expert": e, "space": s}, device_id_type=pl.DeviceIdType.MESH,
        )

    barrier = pltpu.get_barrier_semaphore()

    def greet(e, s):
        pl.semaphore_signal(
            barrier, inc=1, device_id={"expert": e, "space": s}, device_id_type=pl.DeviceIdType.MESH
        )

    @pl.loop(1, NE)
    def _(i):
        greet((me_e + i) % NE, me_s)

    for s in (dev_x1, dev_x3, dev_z1, dev_z2, after, before):
        greet(me_e, s)

    half_rows = WIN // 2
    qw[0] = jnp.zeros((3, HALF, C), BF16)
    qsend[...] = jnp.zeros((3, HALF, C), BF16)
    resid_s[...] = jnp.zeros((TOK, C), BF16)
    cot_s[...] = jnp.zeros((TOK, C), BF16)
    lg_s[...] = jnp.zeros((TOK, EXPERTS), F32)
    ids_s[...] = jnp.full((TOK, 2), -1, I32)
    keep_s[...] = jnp.zeros((TOK, 2), I32)
    for r in range(WIN):
        at = pl.ds(r * PADW, WIN)
        resid_s[at, :] = resid_ref[r]
        cot_s[at, :] = cot_ref[r]
        lg_s[at, :] = logit_ref[r]
        ids_s[at, :] = ids_ref[r]
        keep_s[at, :] = keep_ref[r]
    for r in range(half_rows):
        for k in range(3):
            qsend[k, pl.ds(r * PADW, WIN), :] = attn_ref[k, r]
            qw[0, k, pl.ds(r * PADW, WIN), :] = attn_ref[k, half_rows + r]

    pl.semaphore_wait(barrier, NE - 1 + 6)

    own_w = []
    for m, ref in ((0, up_ref), (1, down_ref)):
        own_w.append(remote(ref, w_all.at[mz, m], w_ss.at[0, m], w_rs.at[0, m], me_e, dev_z2))
    for m, ref in ((0, up_ref), (1, down_ref)):
        own_w.append(remote(ref, w_all.at[mz, m], w_ss.at[1, m], w_rs.at[1, m], me_e, dev_z1))
    halo_q = remote(qsend, qw.at[1], h_ss.at[0], h_rs.at[0], me_e, before)

    resid = resid_s[...].astype(F32)
    rms = jnp.sqrt(jnp.mean(resid * resid, axis=-1, keepdims=True) + NORM_EPS)
    nf = resid / rms
    normed = nf.astype(BF16)
    cot = cot_s[...].astype(F32)
    lg = lg_s[...]
    ids = ids_s[...]
    keep = keep_s[...].astype(F32)
    id1, id2 = ids[:, 0:1], ids[:, 1:2]
    keep1, keep2 = keep[:, 0:1], keep[:, 1:2]
    expert = iota((TOK, EXPERTS), 1)
    oh1 = jnp.where(expert == id1, 1.0, 0.0)
    oh2 = jnp.where(expert == id2, 1.0, 0.0)
    l1 = jnp.sum(jnp.where(expert == id1, lg, 0.0), axis=-1, keepdims=True)
    l2 = jnp.sum(jnp.where(expert == id2, lg, 0.0), axis=-1, keepdims=True)
    lm = jnp.maximum(l1, l2)
    e1, e2 = jnp.exp(l1 - lm), jnp.exp(l2 - lm)
    gate1, gate2 = e1 / (e1 + e2), e2 / (e1 + e2)
    scaled1 = (gate1 * keep1 * cot).astype(BF16)
    scaled2 = (gate2 * keep2 * cot).astype(BF16)
    square_r, square_c = iota((TOK, TOK), 0), iota((TOK, TOK), 1)
    counts = dot(ones_where(square_c < square_r), (oh1 + oh2).astype(BF16))
    slot1 = jnp.sum(oh1 * counts, axis=-1, keepdims=True).astype(I32)
    slot2 = jnp.sum(oh2 * counts, axis=-1, keepdims=True).astype(I32)
    q1 = id1 * CAP + slot1
    q2 = id2 * CAP + slot2
    q1_row = jnp.sum(jnp.where(square_r == square_c, q1, 0), axis=0, keepdims=True)
    q2_row = jnp.sum(jnp.where(square_r == square_c, q2, 0), axis=0, keepdims=True)
    lane = iota((TOK, 128), 1)
    column = jnp.zeros((TOK, 128), F32)
    for i, v in enumerate((gate1, gate2, rms, keep1, keep2)):
        column = jnp.where(lane == i, v, column)
    cols[...] = column

    row = iota((TOK, 1), 0)
    src4 = ge(row, 48) + ge(row, 96) + ge(row, 144)
    rem = row - 48 * src4
    second = ge(rem, 24)

    @pl.loop(0, 4)
    def _(k):
        ch = (2 * (1 - zhi) + k) % 4
        q = (ch * 4 + src4) * 24 + rem - 24 * second
        m1 = q == q1_row
        m2 = q == q2_row
        is_norm = second == 0
        pn = ones_where((m1 | m2) & is_norm)
        ps1 = ones_where(m1 & (second == 1))
        ps2 = ones_where(m2 & (second == 1))
        built = dot(pn, normed) + dot(ps1, scaled1) + dot(ps2, scaled2)
        send_rows[pl.ds(ch * 4, 4)] = built.astype(BF16).reshape(4, 48, C)
        for s in range(4):
            to = ch * 4 + s

            @pl.when(to != me_e)
            def _():
                remote(
                    send_rows.at[to], recv_rows.at[me_e], d_ss.at[to], d_rs.at[me_e], to, me_s
                ).start()

    for cp in own_w:
        cp.start()
    halo_q.start()
    recv_rows[me_e] = send_rows[me_e]

    b96 = ge(row, 96)
    o2 = row - 96 * b96
    b48 = ge(o2, 48)
    o3 = o2 - 48 * b48
    s12 = ge(o3, 12) + ge(o3, 24) + ge(o3, 36)
    perm_s[...] = ones_where(square_c == s12 * 48 + b96 * 24 + b48 * 12 + (o3 - 12 * s12))

    pos_r = square_r % PADW
    pos_c = square_c % PADW
    differ = (pos_r >= half_rows) != (pos_c >= half_rows)
    is_last = me_s == NX * NZ - 1
    last_i = jnp.where(is_last, 1, 0)
    half_differ = (ge(square_r, HALF) != ge(square_c, HALF)) & ((square_r * 0 + last_i) == 1)
    bias = jnp.where(differ | half_differ, SCORE_MASK, 0.0)
    bias_s[...] = jnp.where(pos_c >= WIN, NO_KEY, bias)
    inv_sqrt = (C // HEADS) ** (-0.5)
    halo_q.wait_recv()

    head_lane = iota((1, 128), 1)

    def head_mask(h):
        return ones_where((head_lane >= h * 32) & (head_lane < (h + 1) * 32))

    @pl.loop(0, 4)
    def _(lg_i):
        lanes = pl.ds(pl.multiple_of(lg_i * 128, 128), 128)
        q = jnp.concatenate([qw[0, 0, :, lanes], qw[1, 0, :, lanes]], axis=0)
        k = jnp.concatenate([qw[0, 1, :, lanes], qw[1, 1, :, lanes]], axis=0)
        for h in range(4):
            sc = dot_nt(q * head_mask(h), k) * inv_sqrt + bias_s[...]
            ex = jnp.exp(sc - jnp.max(sc, axis=-1, keepdims=True))
            probs[lg_i * 4 + h] = ex / jnp.sum(ex, axis=-1, keepdims=True)

    @pl.loop(0, 4)
    def _(k):
        grp = (2 * zhi + k) % 4
        for s in range(4):
            frm = grp * 4 + s

            @pl.when(frm != me_e)
            def _():
                remote(
                    send_rows.at[frm], recv_rows.at[frm], d_ss.at[frm], d_rs.at[frm], frm, me_s
                ).wait()

        block = recv_rows[pl.ds(grp * 4, 4)].reshape(TOK, C)
        rows_all[mx, grp] = dot(perm_s[...], block).astype(BF16).reshape(2, 2, 48, C)
        remote(
            rows_all.at[mx, grp], rows_all.at[mx, grp], g_ss.at[0, grp], g_rs.at[0, grp], me_e, dev_x1
        ).start()
        remote(
            rows_all.at[mx, grp], rows_all.at[mx, grp], g_ss.at[1, grp], g_rs.at[1, grp], me_e, dev_x3
        ).start()

    fwd_w = []
    for m in range(2):
        own_w[m].wait_recv()
        cp = remote(
            w_all.at[z2, m], w_all.at[z2, m], w_ss.at[2, m], w_rs.at[2, m], me_e, dev_z1
        )
        cp.start()
        fwd_w.append(cp)

    def x_recv(which, grp):
        frm, dev = ((x1, dev_x1), (x3, dev_x3))[which]
        return remote(
            rows_all.at[frm, grp], rows_all.at[frm, grp], g_ss.at[which, grp], g_rs.at[which, grp],
            me_e, dev,
        )

    fwd_x = []
    for grp in range(4):
        which = 0 if grp < 2 else 1
        x_recv(which, grp).wait_recv()
        frm, dev = ((x1, dev_x3), (x3, dev_x1))[which]
        cp = remote(
            rows_all.at[frm, grp], rows_all.at[frm, grp], g_ss.at[2, grp], g_rs.at[2, grp], me_e, dev
        )
        cp.start()
        fwd_x.append(cp)

    for m in range(2):
        own_w[2 + m].wait_recv()
        fwd_w[m].wait_recv()
    w_all[mz, 0] = up_ref[...]
    w_all[mz, 1] = down_ref[...]
    for m in range(2):
        for j in range(2):
            wcat[m, j] = jnp.concatenate([w_all[c, m, j] for c in range(NZ)], axis=1)

    def expert_rows(b):
        for j in range(2):
            xn = rows_all[b, :, 0, j].reshape(192, C)
            xsc = rows_all[b, :, 1, j].reshape(192, C)
            pre = dot(xn, wcat[0, j])
            sq = pre * pre
            t = jnp.tanh(GELU_C * pre * (1.0 + GELU_A * sq))
            act = (0.5 * pre * (1.0 + t)).astype(BF16)
            slope = 0.5 * (1.0 + t) + 0.5 * GELU_C * pre * (1.0 - t * t) * (1.0 + 3.0 * GELU_A * sq)
            dact = dot(xsc, wcat[1, j])
            dsum = jnp.sum(act.astype(F32) * dact, axis=-1, keepdims=True)
            pg = (dact * slope).astype(BF16)
            act_s[b, j] = act
            pg_s[b, j] = pg
            rg = dot_nt(pg, wcat[0, j])
            part[b, :, pl.ds(j * 48, 48), :] = rg.reshape(4, 48, C)
            hit = iota((48, C), 1) == iota((48, C), 0) + j * 48
            for g in range(4):
                line = jnp.sum(
                    jnp.where(hit, dsum[g * 48 : (g + 1) * 48], 0.0), axis=0, keepdims=True
                )
                if j == 0:
                    tail = jnp.where(iota((16, C), 0) == 0, line, 0.0)
                    part[b, g, pl.ds(96, 16), :] = tail
                else:
                    tail = jnp.where(iota((16, C), 0) == 0, line, 0.0)
                    part[b, g, pl.ds(96, 16), :] += tail

    def x_send(n, dev, slot, sem):
        return remote(xs.at[n], xr.at[slot], x_ss.at[n], x_rs.at[sem], me_e, dev)

    expert_rows(mx)
    x_recv(0, 2).wait_recv()
    x_recv(0, 3).wait_recv()
    expert_rows(x1)
    sums = []
    for g in (0, 1):
        xs[g] = split_tail(part[x1, g])
        sums.append(x_send(g, dev_x1, g, g))
        sums[-1].start()
    x_recv(1, 0).wait_recv()
    x_recv(1, 1).wait_recv()
    expert_rows(x3)
    for g in (2, 3):
        xs[4 + g] = split_tail(part[x3, g])
        sums.append(x_send(4 + g, dev_x3, 4 + g, 4 + g))
        sums[-1].start()
    for cp in fwd_x:
        cp.wait_recv()
    expert_rows(x2)
    for g in (0, 1):
        xs[8 + g] = split_tail(part[x2, g])
        sums.append(x_send(8 + g, dev_x1, 8 + g, 8 + g))
        sums[-1].start()
    for g in (2, 3):
        xs[8 + g] = split_tail(part[x2, g])
        sums.append(x_send(8 + g, dev_x3, 8 + g, 8 + g))
        sums[-1].start()

    def x_got(slot):
        return remote(xs.at[slot], xr.at[slot], x_ss.at[slot], x_rs.at[slot], me_e, dev_x1)

    zsent = []

    def weight_grad(m, j):
        left = rows_all[:, :, m, j].reshape(4 * 192, C)
        right = (pg_s, act_s)[m][:, j].reshape(4 * 192, C)
        full = dot_tn(left, right)
        for c in range(NZ):
            grads[m, j, c] = full[:, c * HID : (c + 1) * HID]
        zsend[0, m, j] = grads[m, j, z3].astype(BF16)
        zsend[1, m, j] = grads[m, j, z1].astype(BF16)
        for n in range(2):
            cp = remote(
                zsend.at[n, m, j], zrecv.at[n, m, j], z_ss.at[n, m, j], z_rs.at[n, m, j], me_e, dev_z1
            )
            cp.start()
            zsent.append(cp)

    def z_forward(m, j):
        zsent[2 * (2 * m + j)].wait_recv()
        zsend[2, m, j] = (grads[m, j, z2] + zrecv[0, m, j].astype(F32)).astype(BF16)
        cp = remote(
            zsend.at[2, m, j], zrecv.at[2, m, j], z_ss.at[2, m, j], z_rs.at[2, m, j], me_e, dev_z2
        )
        cp.start()
        zlast.append(cp)

    zlast = []
    weight_grad(0, 0)
    weight_grad(0, 1)
    for g in (0, 1):
        x_got(8 + g).wait_recv()
        xs[4 + g] = split_tail(part[x3, g] + xr[8 + g].astype(F32))
        sums.append(x_send(4 + g, dev_x3, 4 + g, 4 + g))
        sums[-1].start()
    for g in (2, 3):
        x_got(8 + g).wait_recv()
        xs[g] = split_tail(part[x1, g] + xr[8 + g].astype(F32))
        sums.append(x_send(g, dev_x1, g, g))
        sums[-1].start()
    weight_grad(1, 0)
    weight_grad(1, 1)

    ro = iota((128, 112), 0)
    rs = ge(ro, 32) + ge(ro, 64) + ge(ro, 96)
    rq = ro - 32 * rs
    rj = ge(rq, 12)
    want = jnp.where(rq < 24, rj * 48 + rs * 12 + rq - 12 * rj, jnp.where(rq < 26, rq + 72, -1))
    back = ones_where(iota((128, 112), 1) == want)
    for g in range(4):
        x_got(g).wait_recv()
        x_got(4 + g).wait_recv()
        total = split_tail(part[mx, g] + xr[g].astype(F32) + xr[4 + g].astype(F32))
        ret_send[pl.ds(g * 4, 4)] = dot(back, total).astype(BF16).reshape(4, 32, C)
        for s in range(4):
            to = g * 4 + s

            @pl.when(to != me_e)
            def _():
                remote(
                    ret_send.at[to], ret_recv.at[me_e], r_ss.at[to], r_rs.at[me_e], to, me_s
                ).start()

    ret_recv[me_e] = ret_send[me_e]
    for m in range(2):
        for j in range(2):
            z_forward(m, j)

    @pl.loop(0, NE)
    def _(frm):
        @pl.when(frm != me_e)
        def _():
            remote(
                ret_send.at[frm], ret_recv.at[frm], r_ss.at[frm], r_rs.at[frm], frm, me_s
            ).wait()

    returned = ret_recv[...].reshape(NE * 32, C)
    ids = ids_s[...]
    id1, id2 = ids[:, 0:1], ids[:, 1:2]
    expert = iota((TOK, EXPERTS), 1)
    hot1, hot2 = expert == id1, expert == id2
    oh1, oh2 = jnp.where(hot1, 1.0, 0.0), jnp.where(hot2, 1.0, 0.0)
    counts = dot(ones_where(square_c < square_r), (oh1 + oh2).astype(BF16))
    slot1 = jnp.sum(oh1 * counts, axis=-1, keepdims=True).astype(I32)
    slot2 = jnp.sum(oh2 * counts, axis=-1, keepdims=True).astype(I32)
    q1 = id1 * CAP + slot1
    q2 = id2 * CAP + slot2
    col = iota((TOK, NE * 32), 1)
    dev = lax.shift_right_arithmetic(col, 5)
    pos = col - 32 * dev
    at = dev * 24 + pos
    pick = ones_where(((at == q1) | (at == q2)) & (pos < 24))
    norm_grad = dot(pick, returned)
    rms = cols[:, 2:3]
    resid = resid_s[...].astype(F32)
    nf = resid / rms
    inner = jnp.mean(norm_grad * nf, axis=-1, keepdims=True)
    cot = cot_s[...].astype(F32)
    res_grad = (cot + (norm_grad - nf * inner) / rms).astype(BF16)
    stage[...] = res_grad
    gsend[...] = stage[pl.ds(0, HALF), :]
    halo_g = remote(gsend, gw.at[1], h_ss.at[1], h_rs.at[1], me_e, before)
    halo_g.start()
    gw[0] = stage[pl.ds(HALF, HALF), :]
    for r in range(WIN):
        res_out[r] = stage[pl.ds(r * PADW, WIN), :]

    gate1, gate2 = cols[:, 0:1], cols[:, 1:2]
    keep1, keep2 = cols[:, 3:4], cols[:, 4:5]
    narrow = returned[:, :128]
    tail_pos = (pos == 24) | (pos == 25)

    def gathered(idk, slotk):
        half = lax.shift_right_arithmetic(idk, 1)
        pickk = ones_where((dev == half) & tail_pos)
        found = dot(pickk, narrow)
        spot = (idk - 2 * half) * 48 + (me_e % 4) * 12 + slotk
        return jnp.sum(jnp.where(iota((TOK, 128), 1) == spot, found, 0.0), axis=-1, keepdims=True)

    d1 = gathered(id1, slot1)
    d2 = gathered(id2, slot2)
    part1 = gate2 * d1 - gate1 * d2
    share = jnp.sum(oh1 * keep1 + oh2 * keep2, axis=0, keepdims=True) / (2.0 * WIN * WIN)
    lg = lg_s[...]
    lex = jnp.exp(lg - jnp.max(lg, axis=-1, keepdims=True))
    rp = lex / jnp.sum(lex, axis=-1, keepdims=True)
    share_mean = jnp.sum(rp * share, axis=-1, keepdims=True)
    lg_s[...] = (oh1 - oh2) * part1 + EXPERTS * rp * (share - share_mean)
    for r in range(WIN):
        logit_out[r] = lg_s[pl.ds(r * PADW, WIN), :]

    halo_g.wait_recv()

    @pl.loop(0, 4)
    def _(lg_i):
        lanes = pl.ds(pl.multiple_of(lg_i * 128, 128), 128)
        q = jnp.concatenate([qw[0, 0, :, lanes], qw[1, 0, :, lanes]], axis=0)
        k = jnp.concatenate([qw[0, 1, :, lanes], qw[1, 1, :, lanes]], axis=0)
        v = jnp.concatenate([qw[0, 2, :, lanes], qw[1, 2, :, lanes]], axis=0)
        gs = jnp.concatenate([gw[0, :, lanes], gw[1, :, lanes]], axis=0)
        dq = jnp.zeros((TOK, 128), F32)
        dk = jnp.zeros((TOK, 128), F32)
        dv = jnp.zeros((TOK, 128), F32)
        for h in range(4):
            hm = head_mask(h)
            gm = gs * hm
            pr = probs[lg_i * 4 + h]
            wt = pr.astype(BF16)
            pgrad = dot_nt(gm, v)
            delta = jnp.sum(wt.astype(F32) * pgrad, axis=-1, keepdims=True)
            sg = (pr * (pgrad - delta)).astype(BF16)
            dq = dq + dot(sg, k * hm)
            dk = dk + dot_tn(sg, q * hm)
            dv = dv + dot_tn(wt, gm)
        agrad[0, :, lanes] = (dq * inv_sqrt).astype(BF16)
        agrad[1, :, lanes] = (dk * inv_sqrt).astype(BF16)
        agrad[2, :, lanes] = dv.astype(BF16)

    asend[...] = agrad[:, pl.ds(HALF, HALF), :]
    halo_a = remote(asend, arecv, h_ss.at[2], h_rs.at[2], me_e, after)
    halo_a.start()
    for r in range(half_rows):
        for k in range(3):
            attn_out[k, half_rows + r] = agrad[k, pl.ds(r * PADW, WIN), :]

    for m, out in ((0, up_out), (1, down_out)):
        for j in range(2):
            zsent[2 * (2 * m + j) + 1].wait_recv()
            zlast[2 * m + j].wait_recv()
            out[j] = grads[m, j, mz] + zrecv[1, m, j].astype(F32) + zrecv[2, m, j].astype(F32)

    halo_a.wait_recv()
    for r in range(half_rows):
        for k in range(3):
            attn_out[k, r] = arecv[k, pl.ds(r * PADW, WIN), :]

    for cp in (*own_w, *fwd_w, *fwd_x, *sums, *zsent, *zlast, halo_q, halo_g, halo_a):
        cp.wait_send()
    for grp in range(4):
        for which in range(2):
            x_recv(which, grp).wait_send()


def per_device(attn_inputs, residual, logits, expert_ids, keep_mask, cotangent, up_weight, down_weight):
    vmem = pl.BlockSpec(memory_space=pltpu.VMEM)
    dma = pltpu.SemaphoreType.DMA
    outs = pl.pallas_call(
        kernel,
        out_shape=(
            jax.ShapeDtypeStruct((3, WIN, WIN, C), BF16),
            jax.ShapeDtypeStruct((WIN, WIN, C), BF16),
            jax.ShapeDtypeStruct((2, C, HID), F32),
            jax.ShapeDtypeStruct((2, C, HID), F32),
            jax.ShapeDtypeStruct((WIN, WIN, EXPERTS), F32),
        ),
        in_specs=[vmem] * 8,
        out_specs=(vmem,) * 5,
        scratch_shapes=[
            pltpu.VMEM((2, 3, HALF, C), BF16),
            pltpu.VMEM((3, HALF, C), BF16),
            pltpu.VMEM((2, HALF, C), BF16),
            pltpu.VMEM((HALF, C), BF16),
            pltpu.VMEM((3, TOK, C), BF16),
            pltpu.VMEM((3, HALF, C), BF16),
            pltpu.VMEM((3, HALF, C), BF16),
            pltpu.VMEM((TOK, C), BF16),
            pltpu.VMEM((TOK, C), BF16),
            pltpu.VMEM((TOK, EXPERTS), F32),
            pltpu.VMEM((TOK, 2), I32),
            pltpu.VMEM((TOK, 2), I32),
            pltpu.VMEM((TOK, 128), F32),
            pltpu.VMEM((TOK, C), BF16),
            pltpu.VMEM((HEADS, TOK, TOK), F32),
            pltpu.VMEM((TOK, TOK), BF16),
            pltpu.VMEM((TOK, TOK), F32),
            pltpu.VMEM((NE, 48, C), BF16),
            pltpu.VMEM((NE, 48, C), BF16),
            pltpu.VMEM((NX, 4, 2, 2, 48, C), BF16),
            pltpu.VMEM((NZ, 2, 2, C, HID), BF16),
            pltpu.VMEM((2, 2, C, NZ * HID), BF16),
            pltpu.VMEM((NX, 2, 192, NZ * HID), BF16),
            pltpu.VMEM((NX, 2, 192, NZ * HID), BF16),
            pltpu.VMEM((NX, 4, 112, C), F32),
            pltpu.VMEM((12, 112, C), BF16),
            pltpu.VMEM((12, 112, C), BF16),
            pltpu.VMEM((NE, 32, C), BF16),
            pltpu.VMEM((NE, 32, C), BF16),
            pltpu.VMEM((2, 2, NZ, C, HID), F32),
            pltpu.VMEM((3, 2, 2, C, HID), BF16),
            pltpu.VMEM((3, 2, 2, C, HID), BF16),
            dma((NE,)), dma((NE,)),
            dma((3, 4)), dma((3, 4)),
            dma((3, 2)), dma((3, 2)),
            dma((12,)), dma((12,)),
            dma((NE,)), dma((NE,)),
            dma((3, 2, 2)), dma((3, 2, 2)),
            dma((3,)), dma((3,)),
        ],
        compiler_params=pltpu.CompilerParams(
            collective_id=0, has_side_effects=True, vmem_limit_bytes=56 * 1024 * 1024
        ),
    )(
        attn_inputs[:, 0], residual[0], logits[0], expert_ids[0], keep_mask[0], cotangent[0],
        up_weight, down_weight,
    )
    attn_grad, res_grad, up_grad, down_grad, logit_grad = outs
    return attn_grad[:, None], res_grad[None], up_grad, down_grad, logit_grad[None]


def solution(mesh):
    in_specs = (
        P(None, "expert", "space", None, None),
        P("expert", "space", None, None),
        P("expert", "space", None, None),
        P("expert", "space", None, None),
        P("expert", "space", None, None),
        P("expert", "space", None, None),
        P("expert", None, "space"),
        P("expert", None, "space"),
    )
    out_specs = (
        P(None, "expert", "space", None, None),
        P("expert", "space", None, None),
        P("expert", None, "space"),
        P("expert", None, "space"),
        P("expert", "space", None, None),
    )
    return jax.shard_map(
        per_device, mesh=mesh, in_specs=in_specs, out_specs=out_specs, check_vma=False
    )
```

```python
import jax
import jax.numpy as jnp
from jax import lax
from jax.experimental import pallas as pl
from jax.experimental.pallas import tpu as pltpu
from jax.sharding import PartitionSpec as P

WIN = 12
PADW = 16
TOK = WIN * PADW
HALF = TOK // 2
C = 512
HEADS = 16
EXPERTS = 32
CAP = 12
NE = 16
NX = 4
NZ = 4
RING = 8
NYC = 8
HID = 128
NORM_EPS = 1e-06
SCORE_MASK = -100.0
NO_KEY = -1e30
GELU_C = 0.7978845608028654
GELU_A = 0.044715
F32 = jnp.float32
BF16 = jnp.bfloat16
I32 = jnp.int32


def iota(shape, dim):
    return lax.broadcasted_iota(I32, shape, dim)


def dot(a, b):
    return lax.dot_general(a, b, (((1,), (0,)), ((), ())), preferred_element_type=F32)


def dot_nt(a, b):
    return lax.dot_general(a, b, (((1,), (1,)), ((), ())), preferred_element_type=F32)


def dot_tn(a, b):
    return lax.dot_general(a, b, (((0,), (0,)), ((), ())), preferred_element_type=F32)


def ge(a, n):
    return (a >= n).astype(I32)


def ones_where(cond):
    return jnp.where(cond, 1.0, 0.0).astype(BF16)


def split_tail(x):
    total = x[96:97] + x[97:98]
    high = total.astype(BF16).astype(F32)
    low = total - high
    row = iota((16, C), 0)
    tail = jnp.where(row == 0, high, jnp.where(row == 1, low, 0.0))
    return jnp.concatenate([x[:96], tail], axis=0).astype(BF16)


def kernel(
    attn_ref, resid_ref, logit_ref, ids_ref, keep_ref, cot_ref, up_ref, down_ref,
    attn_out, res_out, up_out, down_out, logit_out,
    qw, qsend, gw, gsend, agrad, asend, arecv,
    resid_s, cot_s, lg_s, ids_s, keep_s, cols, stage, probs, perm_s, bias_s,
    send_rows, recv_rows, rows_all, w_all, wcat, pg_s, act_s, part, xs, xr,
    ret_send, ret_recv, grads, zsend, zrecv,
    d_ss, d_rs, g_ss, g_rs, w_ss, w_rs, x_ss, x_rs, r_ss, r_rs, z_ss, z_rs, h_ss, h_rs,
):
    me_e = lax.axis_index("expert")
    me_s = lax.axis_index("space")
    mx = me_s // NZ
    mz = me_s % NZ
    zhi = me_e // 8
    x1 = mx + 1 - 2 * (mx % 2)
    x3 = NX - 1 - mx
    x2 = NX - 1 - x1
    me_yc = me_e % NYC
    zr = zhi * NZ + mz
    dev_x1 = x1 * NZ + mz
    dev_x3 = x3 * NZ + mz
    ring = []
    for step in (1, RING - 1):
        to = (zr + step) % RING
        ring.append(((to // NZ) * NYC + me_yc, mx * NZ + to % NZ))
    after = (me_s + 1) % (NX * NZ)
    before = (me_s + NX * NZ - 1) % (NX * NZ)

    def remote(src, dst, ss, rs, e, s):
        return pltpu.make_async_remote_copy(
            src_ref=src, dst_ref=dst, send_sem=ss, recv_sem=rs,
            device_id={"expert": e, "space": s}, device_id_type=pl.DeviceIdType.MESH,
        )

    barrier = pltpu.get_barrier_semaphore()

    def greet(e, s):
        pl.semaphore_signal(
            barrier, inc=1, device_id={"expert": e, "space": s}, device_id_type=pl.DeviceIdType.MESH
        )

    @pl.loop(1, NYC)
    def _(i):
        greet(zhi * NYC + (me_yc + i) % NYC, me_s)

    for e, s in ring:
        greet(e, s)
    for s in (dev_x1, dev_x3, after, before):
        greet(me_e, s)

    half_rows = WIN // 2
    qw[0] = jnp.zeros((3, HALF, C), BF16)
    qsend[...] = jnp.zeros((3, HALF, C), BF16)
    resid_s[...] = jnp.zeros((TOK, C), BF16)
    cot_s[...] = jnp.zeros((TOK, C), BF16)
    lg_s[...] = jnp.zeros((TOK, EXPERTS), F32)
    ids_s[...] = jnp.full((TOK, 2), -1, I32)
    keep_s[...] = jnp.zeros((TOK, 2), I32)
    for r in range(WIN):
        at = pl.ds(r * PADW, WIN)
        resid_s[at, :] = resid_ref[r]
        cot_s[at, :] = cot_ref[r]
        lg_s[at, :] = logit_ref[r]
        ids_s[at, :] = ids_ref[r]
        keep_s[at, :] = keep_ref[r]
    for r in range(half_rows):
        for k in range(3):
            qsend[k, pl.ds(r * PADW, WIN), :] = attn_ref[k, r]
            qw[0, k, pl.ds(r * PADW, WIN), :] = attn_ref[k, half_rows + r]

    pl.semaphore_wait(barrier, NYC - 1 + 6)

    def weight_copy(way, step, m, j):
        chunk = (zr - step) % RING if way == 0 else (zr + step) % RING
        src = (up_ref, down_ref)[m].at[j] if step == 0 else w_all.at[chunk, m, j]
        return remote(
            src, w_all.at[chunk, m, j], w_ss.at[way, step, m, j], w_rs.at[way, step, m, j], *ring[way]
        )

    def weight_arrived(way, step, m, j):
        chunk = (zr - 1 - step) % RING if way == 0 else (zr + 1 + step) % RING
        remote(
            w_all.at[chunk, m, j], w_all.at[chunk, m, j], w_ss.at[way, step, m, j],
            w_rs.at[way, step, m, j], *ring[way],
        ).wait_recv()

    pieces = [(m, j) for m in range(2) for j in range(2)]
    sent_w = []

    def start_weight(way, step, m, j):
        cp = weight_copy(way, step, m, j)
        cp.start()
        sent_w.append(cp)

    def forward_weights(step):
        for m, j in pieces:
            for way in range(2):
                weight_arrived(way, step - 1, m, j)
                if step < 3 or m == way:
                    start_weight(way, step, m, j)

    for m, j in pieces:
        for way in range(2):
            start_weight(way, 0, m, j)
    halo_q = remote(qsend, qw.at[1], h_ss.at[0], h_rs.at[0], me_e, before)

    resid = resid_s[...].astype(F32)
    rms = jnp.sqrt(jnp.mean(resid * resid, axis=-1, keepdims=True) + NORM_EPS)
    nf = resid / rms
    normed = nf.astype(BF16)
    cot = cot_s[...].astype(F32)
    lg = lg_s[...]
    ids = ids_s[...]
    keep = keep_s[...].astype(F32)
    id1, id2 = ids[:, 0:1], ids[:, 1:2]
    keep1, keep2 = keep[:, 0:1], keep[:, 1:2]
    expert = iota((TOK, EXPERTS), 1)
    oh1 = jnp.where(expert == id1, 1.0, 0.0)
    oh2 = jnp.where(expert == id2, 1.0, 0.0)
    l1 = jnp.sum(jnp.where(expert == id1, lg, 0.0), axis=-1, keepdims=True)
    l2 = jnp.sum(jnp.where(expert == id2, lg, 0.0), axis=-1, keepdims=True)
    lm = jnp.maximum(l1, l2)
    e1, e2 = jnp.exp(l1 - lm), jnp.exp(l2 - lm)
    gate1, gate2 = e1 / (e1 + e2), e2 / (e1 + e2)
    scaled1 = (gate1 * keep1 * cot).astype(BF16)
    scaled2 = (gate2 * keep2 * cot).astype(BF16)
    square_r, square_c = iota((TOK, TOK), 0), iota((TOK, TOK), 1)
    counts = dot(ones_where(square_c < square_r), (oh1 + oh2).astype(BF16))
    slot1 = jnp.sum(oh1 * counts, axis=-1, keepdims=True).astype(I32)
    slot2 = jnp.sum(oh2 * counts, axis=-1, keepdims=True).astype(I32)
    q1 = id1 * CAP + slot1
    q2 = id2 * CAP + slot2
    q1_row = jnp.sum(jnp.where(square_r == square_c, q1, 0), axis=0, keepdims=True)
    q2_row = jnp.sum(jnp.where(square_r == square_c, q2, 0), axis=0, keepdims=True)
    lane = iota((TOK, 128), 1)
    column = jnp.zeros((TOK, 128), F32)
    for i, v in enumerate((gate1, gate2, rms, keep1, keep2)):
        column = jnp.where(lane == i, v, column)
    cols[...] = column

    row = iota((TOK, 1), 0)
    src4 = ge(row, 48) + ge(row, 96) + ge(row, 144)
    rem = row - 48 * src4
    second = ge(rem, 24)

    @pl.loop(0, 2)
    def _(h):
        for p in range(2):
            q = (p * NYC + h * 4 + src4) * 24 + rem - 24 * second
            m1 = q == q1_row
            m2 = q == q2_row
            pn = ones_where((m1 | m2) & (second == 0))
            ps1 = ones_where(m1 & (second == 1))
            ps2 = ones_where(m2 & (second == 1))
            built = dot(pn, normed) + dot(ps1, scaled1) + dot(ps2, scaled2)
            send_rows[pl.ds(h * 4, 4), p] = built.astype(BF16).reshape(4, 48, C)
        for s in range(4):
            to = h * 4 + s

            @pl.when(to != me_yc)
            def _():
                remote(
                    send_rows.at[to], recv_rows.at[me_yc], d_ss.at[to], d_rs.at[me_yc],
                    zhi * NYC + to, me_s,
                ).start()

    halo_q.start()
    recv_rows[me_yc] = send_rows[me_yc]

    b96 = ge(row, 96)
    o2 = row - 96 * b96
    b48 = ge(o2, 48)
    o3 = o2 - 48 * b48
    s12 = ge(o3, 12) + ge(o3, 24) + ge(o3, 36)
    perm_s[...] = ones_where(square_c == s12 * 48 + b96 * 24 + b48 * 12 + (o3 - 12 * s12))

    pos_r = square_r % PADW
    pos_c = square_c % PADW
    differ = (pos_r >= half_rows) != (pos_c >= half_rows)
    is_last = me_s == NX * NZ - 1
    last_i = jnp.where(is_last, 1, 0)
    half_differ = (ge(square_r, HALF) != ge(square_c, HALF)) & ((square_r * 0 + last_i) == 1)
    bias = jnp.where(differ | half_differ, SCORE_MASK, 0.0)
    bias_s[...] = jnp.where(pos_c >= WIN, NO_KEY, bias)
    inv_sqrt = (C // HEADS) ** (-0.5)
    halo_q.wait_recv()

    head_lane = iota((1, 128), 1)

    def head_mask(h):
        return ones_where((head_lane >= h * 32) & (head_lane < (h + 1) * 32))

    @pl.loop(0, 4)
    def _(lg_i):
        lanes = pl.ds(pl.multiple_of(lg_i * 128, 128), 128)
        q = jnp.concatenate([qw[0, 0, :, lanes], qw[1, 0, :, lanes]], axis=0)
        k = jnp.concatenate([qw[0, 1, :, lanes], qw[1, 1, :, lanes]], axis=0)
        for h in range(4):
            sc = dot_nt(q * head_mask(h), k) * inv_sqrt + bias_s[...]
            ex = jnp.exp(sc - jnp.max(sc, axis=-1, keepdims=True))
            probs[lg_i * 4 + h] = ex / jnp.sum(ex, axis=-1, keepdims=True)

    @pl.loop(0, 2)
    def _(g):
        for s in range(4):
            frm = g * 4 + s

            @pl.when(frm != me_yc)
            def _():
                remote(
                    send_rows.at[frm], recv_rows.at[frm], d_ss.at[frm], d_rs.at[frm],
                    zhi * NYC + frm, me_s,
                ).wait()

        for p in range(2):
            grp = 2 * p + g
            block = recv_rows[pl.ds(g * 4, 4), p].reshape(TOK, C)
            rows_all[mx, grp] = dot(perm_s[...], block).astype(BF16).reshape(2, 2, 48, C)
            for which, dev in ((0, dev_x1), (1, dev_x3)):
                remote(
                    rows_all.at[mx, grp], rows_all.at[mx, grp], g_ss.at[which, grp],
                    g_rs.at[which, grp], me_e, dev,
                ).start()

    forward_weights(1)
    w_all[zr, 0] = up_ref[...]
    w_all[zr, 1] = down_ref[...]

    def x_recv(which, grp):
        frm, dev = ((x1, dev_x1), (x3, dev_x3))[which]
        return remote(
            rows_all.at[frm, grp], rows_all.at[frm, grp], g_ss.at[which, grp], g_rs.at[which, grp],
            me_e, dev,
        )

    fwd_x = []

    def forward_rows(grp):
        which = 0 if grp < 2 else 1
        x_recv(which, grp).wait_recv()
        frm, dev = ((x1, dev_x3), (x3, dev_x1))[which]
        cp = remote(
            rows_all.at[frm, grp], rows_all.at[frm, grp], g_ss.at[2, grp], g_rs.at[2, grp], me_e, dev
        )
        cp.start()
        fwd_x.append(cp)

    forward_rows(0)
    forward_rows(2)
    forward_weights(2)
    forward_rows(1)
    forward_rows(3)
    forward_weights(3)
    for way in range(2):
        for j in range(2):
            weight_arrived(way, 3, way, j)
    for grp in (2, 3):
        x_recv(0, grp).wait_recv()
    for grp in (0, 1):
        x_recv(1, grp).wait_recv()
    for cp in fwd_x:
        cp.wait_recv()

    def expert_rows(p):
        for m, j in pieces:
            wcat[m, j] = jnp.concatenate([w_all[p * NZ + c, m, j] for c in range(NZ)], axis=1)
        for j in range(2):
            xn = rows_all[:, pl.ds(2 * p, 2), 0, j].reshape(384, C)
            xsc = rows_all[:, pl.ds(2 * p, 2), 1, j].reshape(384, C)
            pre = dot(xn, wcat[0, j])
            sq = pre * pre
            t = jnp.tanh(GELU_C * pre * (1.0 + GELU_A * sq))
            act = (0.5 * pre * (1.0 + t)).astype(BF16)
            slope = 0.5 * (1.0 + t) + 0.5 * GELU_C * pre * (1.0 - t * t) * (1.0 + 3.0 * GELU_A * sq)
            dact = dot(xsc, wcat[1, j])
            dsum = jnp.sum(act.astype(F32) * dact, axis=-1, keepdims=True)
            pg = (dact * slope).astype(BF16)
            act_s[j] = act
            pg_s[j] = pg
            rg = dot_nt(pg, wcat[0, j])
            part[:, pl.ds(2 * p, 2), pl.ds(j * 48, 48), :] = rg.reshape(4, 2, 48, C)
            hit = iota((48, C), 1) == iota((48, C), 0) + j * 48
            for b in range(NX):
                for g in range(2):
                    lo = (2 * b + g) * 48
                    line = jnp.sum(jnp.where(hit, dsum[lo : lo + 48], 0.0), axis=0, keepdims=True)
                    tail = jnp.where(iota((16, C), 0) == 0, line, 0.0)
                    if j == 0:
                        part[b, 2 * p + g, pl.ds(96, 16), :] = tail
                    else:
                        part[b, 2 * p + g, pl.ds(96, 16), :] += tail

    def expert_grads(p):
        for m, j in pieces:
            left = rows_all[:, pl.ds(2 * p, 2), m, j].reshape(384, C)
            full = dot_tn(left, (pg_s, act_s)[m][j])
            for c in range(NZ):
                grads[p * NZ + c, m, j] = full[:, c * HID : (c + 1) * HID]

    def x_send(n, dev, slot, sem):
        return remote(xs.at[n], xr.at[slot], x_ss.at[n], x_rs.at[sem], me_e, dev)

    sent_z = []

    def start_sum(way, step, m, j, add):
        to = (zr + 4 - step) % RING if way == 0 else (zr + 4 + step) % RING
        value = grads[to, m, j]
        if add:
            cp = remote(
                zsend.at[way, step - 1, m, j], zrecv.at[way, step - 1, m, j],
                z_ss.at[way, step - 1, m, j], z_rs.at[way, step - 1, m, j], *ring[way],
            )
            cp.wait_recv()
            value = value + zrecv[way, step - 1, m, j].astype(F32)
        zsend[way, step, m, j] = value.astype(BF16)
        cp = remote(
            zsend.at[way, step, m, j], zrecv.at[way, step, m, j], z_ss.at[way, step, m, j],
            z_rs.at[way, step, m, j], *ring[way],
        )
        cp.start()
        sent_z.append(cp)

    def x_got(slot):
        return remote(xs.at[slot], xr.at[slot], x_ss.at[slot], x_rs.at[slot], me_e, dev_x1)

    sums = []
    def send_sum(slot, dev, value):
        xs[slot] = split_tail(value)
        sums.append(x_send(slot, dev, slot, slot))
        sums[-1].start()

    expert_rows(1 - zhi)
    expert_grads(1 - zhi)
    for m, j in pieces:
        start_sum(m, 0, m, j, False)
    expert_rows(zhi)
    for g in (0, 1):
        send_sum(8 + g, dev_x1, part[x2, g])
        send_sum(10 + g, dev_x3, part[x2, 2 + g])
    for g in (0, 1):
        send_sum(g, dev_x1, part[x1, g])
        send_sum(6 + g, dev_x3, part[x3, 2 + g])
    expert_grads(zhi)
    for m, j in pieces:
        start_sum(1 - m, 1, m, j, False)
    for m, j in pieces:
        start_sum(m, 1, m, j, True)
    for g in (0, 1):
        x_got(8 + g).wait_recv()
        send_sum(4 + g, dev_x3, part[x3, g] + xr[8 + g].astype(F32))
        x_got(10 + g).wait_recv()
        send_sum(2 + g, dev_x1, part[x1, 2 + g] + xr[10 + g].astype(F32))

    ro = iota((128, 112), 0)
    rs = ge(ro, 32) + ge(ro, 64) + ge(ro, 96)
    rq = ro - 32 * rs
    rj = ge(rq, 12)
    want = jnp.where(rq < 24, rj * 48 + rs * 12 + rq - 12 * rj, jnp.where(rq < 26, rq + 72, -1))
    back = ones_where(iota((128, 112), 1) == want)
    for g in range(2):
        for p in range(2):
            grp = 2 * p + g
            x_got(grp).wait_recv()
            x_got(4 + grp).wait_recv()
            total = split_tail(part[mx, grp] + xr[grp].astype(F32) + xr[4 + grp].astype(F32))
            ret_send[pl.ds(g * 4, 4), p] = dot(back, total).astype(BF16).reshape(4, 32, C)
        for s in range(4):
            to = g * 4 + s

            @pl.when(to != me_yc)
            def _():
                remote(
                    ret_send.at[to], ret_recv.at[me_yc], r_ss.at[to], r_rs.at[me_yc],
                    zhi * NYC + to, me_s,
                ).start()

    ret_recv[me_yc] = ret_send[me_yc]
    for m, j in pieces:
        for way in range(2):
            start_sum(way, 2, m, j, True)

    @pl.loop(0, NYC)
    def _(frm):
        @pl.when(frm != me_yc)
        def _():
            remote(
                ret_send.at[frm], ret_recv.at[frm], r_ss.at[frm], r_rs.at[frm],
                zhi * NYC + frm, me_s,
            ).wait()

    returned = ret_recv[...].reshape(NE * 32, C)
    ids = ids_s[...]
    id1, id2 = ids[:, 0:1], ids[:, 1:2]
    expert = iota((TOK, EXPERTS), 1)
    hot1, hot2 = expert == id1, expert == id2
    oh1, oh2 = jnp.where(hot1, 1.0, 0.0), jnp.where(hot2, 1.0, 0.0)
    counts = dot(ones_where(square_c < square_r), (oh1 + oh2).astype(BF16))
    slot1 = jnp.sum(oh1 * counts, axis=-1, keepdims=True).astype(I32)
    slot2 = jnp.sum(oh2 * counts, axis=-1, keepdims=True).astype(I32)
    q1 = id1 * CAP + slot1
    q2 = id2 * CAP + slot2
    col = iota((TOK, NE * 32), 1)
    block_of = lax.shift_right_arithmetic(col, 5)
    pos = col - 32 * block_of
    dev = lax.shift_right_arithmetic(block_of, 1) + NYC * (block_of % 2)
    at = dev * 24 + pos
    pick = ones_where(((at == q1) | (at == q2)) & (pos < 24))
    norm_grad = dot(pick, returned)
    rms = cols[:, 2:3]
    resid = resid_s[...].astype(F32)
    nf = resid / rms
    inner = jnp.mean(norm_grad * nf, axis=-1, keepdims=True)
    cot = cot_s[...].astype(F32)
    res_grad = (cot + (norm_grad - nf * inner) / rms).astype(BF16)
    stage[...] = res_grad
    gsend[...] = stage[pl.ds(0, HALF), :]
    halo_g = remote(gsend, gw.at[1], h_ss.at[1], h_rs.at[1], me_e, before)
    halo_g.start()
    gw[0] = stage[pl.ds(HALF, HALF), :]
    for r in range(WIN):
        res_out[r] = stage[pl.ds(r * PADW, WIN), :]

    gate1, gate2 = cols[:, 0:1], cols[:, 1:2]
    keep1, keep2 = cols[:, 3:4], cols[:, 4:5]
    narrow = returned[:, :128]
    tail_pos = (pos == 24) | (pos == 25)

    def gathered(idk, slotk):
        half = lax.shift_right_arithmetic(idk, 1)
        pickk = ones_where((dev == half) & tail_pos)
        found = dot(pickk, narrow)
        spot = (idk - 2 * half) * 48 + (me_e % 4) * 12 + slotk
        return jnp.sum(jnp.where(iota((TOK, 128), 1) == spot, found, 0.0), axis=-1, keepdims=True)

    d1 = gathered(id1, slot1)
    d2 = gathered(id2, slot2)
    part1 = gate2 * d1 - gate1 * d2
    share = jnp.sum(oh1 * keep1 + oh2 * keep2, axis=0, keepdims=True) / (2.0 * WIN * WIN)
    lg = lg_s[...]
    lex = jnp.exp(lg - jnp.max(lg, axis=-1, keepdims=True))
    rp = lex / jnp.sum(lex, axis=-1, keepdims=True)
    share_mean = jnp.sum(rp * share, axis=-1, keepdims=True)
    lg_s[...] = (oh1 - oh2) * part1 + EXPERTS * rp * (share - share_mean)
    for r in range(WIN):
        logit_out[r] = lg_s[pl.ds(r * PADW, WIN), :]

    for m, j in pieces:
        for way in range(2):
            start_sum(way, 3, m, j, True)

    halo_g.wait_recv()

    @pl.loop(0, 4)
    def _(lg_i):
        lanes = pl.ds(pl.multiple_of(lg_i * 128, 128), 128)
        q = jnp.concatenate([qw[0, 0, :, lanes], qw[1, 0, :, lanes]], axis=0)
        k = jnp.concatenate([qw[0, 1, :, lanes], qw[1, 1, :, lanes]], axis=0)
        v = jnp.concatenate([qw[0, 2, :, lanes], qw[1, 2, :, lanes]], axis=0)
        gs = jnp.concatenate([gw[0, :, lanes], gw[1, :, lanes]], axis=0)
        dq = jnp.zeros((TOK, 128), F32)
        dk = jnp.zeros((TOK, 128), F32)
        dv = jnp.zeros((TOK, 128), F32)
        for h in range(4):
            hm = head_mask(h)
            gm = gs * hm
            pr = probs[lg_i * 4 + h]
            wt = pr.astype(BF16)
            pgrad = dot_nt(gm, v)
            delta = jnp.sum(wt.astype(F32) * pgrad, axis=-1, keepdims=True)
            sg = (pr * (pgrad - delta)).astype(BF16)
            dq = dq + dot(sg, k * hm)
            dk = dk + dot_tn(sg, q * hm)
            dv = dv + dot_tn(wt, gm)
        agrad[0, :, lanes] = (dq * inv_sqrt).astype(BF16)
        agrad[1, :, lanes] = (dk * inv_sqrt).astype(BF16)
        agrad[2, :, lanes] = dv.astype(BF16)

    asend[...] = agrad[:, pl.ds(HALF, HALF), :]
    halo_a = remote(asend, arecv, h_ss.at[2], h_rs.at[2], me_e, after)
    halo_a.start()
    for r in range(half_rows):
        for k in range(3):
            attn_out[k, half_rows + r] = agrad[k, pl.ds(r * PADW, WIN), :]

    for m, out in ((0, up_out), (1, down_out)):
        for j in range(2):
            value = grads[zr, m, j]
            for way in range(2):
                remote(
                    zsend.at[way, 3, m, j], zrecv.at[way, 3, m, j], z_ss.at[way, 3, m, j],
                    z_rs.at[way, 3, m, j], *ring[way],
                ).wait_recv()
                value = value + zrecv[way, 3, m, j].astype(F32)
            out[j] = value

    halo_a.wait_recv()
    for r in range(half_rows):
        for k in range(3):
            attn_out[k, r] = arecv[k, pl.ds(r * PADW, WIN), :]

    for cp in (*sent_w, *fwd_x, *sums, *sent_z, halo_q, halo_g, halo_a):
        cp.wait_send()
    for grp in range(4):
        for which in range(2):
            x_recv(which, grp).wait_send()


def per_device(attn_inputs, residual, logits, expert_ids, keep_mask, cotangent, up_weight, down_weight):
    vmem = pl.BlockSpec(memory_space=pltpu.VMEM)
    dma = pltpu.SemaphoreType.DMA
    outs = pl.pallas_call(
        kernel,
        out_shape=(
            jax.ShapeDtypeStruct((3, WIN, WIN, C), BF16),
            jax.ShapeDtypeStruct((WIN, WIN, C), BF16),
            jax.ShapeDtypeStruct((2, C, HID), F32),
            jax.ShapeDtypeStruct((2, C, HID), F32),
            jax.ShapeDtypeStruct((WIN, WIN, EXPERTS), F32),
        ),
        in_specs=[vmem] * 8,
        out_specs=(vmem,) * 5,
        scratch_shapes=[
            pltpu.VMEM((2, 3, HALF, C), BF16),
            pltpu.VMEM((3, HALF, C), BF16),
            pltpu.VMEM((2, HALF, C), BF16),
            pltpu.VMEM((HALF, C), BF16),
            pltpu.VMEM((3, TOK, C), BF16),
            pltpu.VMEM((3, HALF, C), BF16),
            pltpu.VMEM((3, HALF, C), BF16),
            pltpu.VMEM((TOK, C), BF16),
            pltpu.VMEM((TOK, C), BF16),
            pltpu.VMEM((TOK, EXPERTS), F32),
            pltpu.VMEM((TOK, 2), I32),
            pltpu.VMEM((TOK, 2), I32),
            pltpu.VMEM((TOK, 128), F32),
            pltpu.VMEM((TOK, C), BF16),
            pltpu.VMEM((HEADS, TOK, TOK), F32),
            pltpu.VMEM((TOK, TOK), BF16),
            pltpu.VMEM((TOK, TOK), F32),
            pltpu.VMEM((NYC, 2, 48, C), BF16),
            pltpu.VMEM((NYC, 2, 48, C), BF16),
            pltpu.VMEM((NX, 4, 2, 2, 48, C), BF16),
            pltpu.VMEM((RING, 2, 2, C, HID), BF16),
            pltpu.VMEM((2, 2, C, NZ * HID), BF16),
            pltpu.VMEM((2, 384, NZ * HID), BF16),
            pltpu.VMEM((2, 384, NZ * HID), BF16),
            pltpu.VMEM((NX, 4, 112, C), F32),
            pltpu.VMEM((12, 112, C), BF16),
            pltpu.VMEM((12, 112, C), BF16),
            pltpu.VMEM((NYC, 2, 32, C), BF16),
            pltpu.VMEM((NYC, 2, 32, C), BF16),
            pltpu.VMEM((RING, 2, 2, C, HID), F32),
            pltpu.VMEM((2, 4, 2, 2, C, HID), BF16),
            pltpu.VMEM((2, 4, 2, 2, C, HID), BF16),
            dma((NYC,)), dma((NYC,)),
            dma((3, 4)), dma((3, 4)),
            dma((2, 4, 2, 2)), dma((2, 4, 2, 2)),
            dma((12,)), dma((12,)),
            dma((NYC,)), dma((NYC,)),
            dma((2, 4, 2, 2)), dma((2, 4, 2, 2)),
            dma((3,)), dma((3,)),
        ],
        compiler_params=pltpu.CompilerParams(
            collective_id=0, has_side_effects=True, vmem_limit_bytes=56 * 1024 * 1024
        ),
    )(
        attn_inputs[:, 0], residual[0], logits[0], expert_ids[0], keep_mask[0], cotangent[0],
        up_weight, down_weight,
    )
    attn_grad, res_grad, up_grad, down_grad, logit_grad = outs
    return attn_grad[:, None], res_grad[None], up_grad, down_grad, logit_grad[None]


def solution(mesh):
    in_specs = (
        P(None, "expert", "space", None, None),
        P("expert", "space", None, None),
        P("expert", "space", None, None),
        P("expert", "space", None, None),
        P("expert", "space", None, None),
        P("expert", "space", None, None),
        P("expert", None, "space"),
        P("expert", None, "space"),
    )
    out_specs = (
        P(None, "expert", "space", None, None),
        P("expert", "space", None, None),
        P("expert", None, "space"),
        P("expert", None, "space"),
        P("expert", "space", None, None),
    )
    return jax.shard_map(
        per_device, mesh=mesh, in_specs=in_specs, out_specs=out_specs, check_vma=False
    )
```

```python
import jax
import jax.numpy as jnp
from jax import lax
from jax.experimental import pallas as pl
from jax.experimental.pallas import tpu as pltpu
from jax.sharding import PartitionSpec as P

WIN = 12
PADW = 16
TOK = WIN * PADW
HALF = TOK // 2
C = 512
HEADS = 16
EXPERTS = 32
CAP = 12
NE = 16
NX = 4
NZ = 4
RING = 8
NYC = 8
HID = 128
NORM_EPS = 1e-06
SCORE_MASK = -100.0
NO_KEY = -1e30
GELU_C = 0.7978845608028654
GELU_A = 0.044715
F32 = jnp.float32
BF16 = jnp.bfloat16
I32 = jnp.int32


def iota(shape, dim):
    return lax.broadcasted_iota(I32, shape, dim)


def dot(a, b):
    return lax.dot_general(a, b, (((1,), (0,)), ((), ())), preferred_element_type=F32)


def dot_nt(a, b):
    return lax.dot_general(a, b, (((1,), (1,)), ((), ())), preferred_element_type=F32)


def dot_tn(a, b):
    return lax.dot_general(a, b, (((0,), (0,)), ((), ())), preferred_element_type=F32)


def ge(a, n):
    return (a >= n).astype(I32)


def ones_where(cond):
    return jnp.where(cond, 1.0, 0.0).astype(BF16)


def split_tail(x):
    total = x[48:49] + x[49:50]
    high = total.astype(BF16).astype(F32)
    low = total - high
    row = iota((16, C), 0)
    tail = jnp.where(row == 0, high, jnp.where(row == 1, low, 0.0))
    return jnp.concatenate([x[:48], tail], axis=0).astype(BF16)


def kernel(
    attn_ref, resid_ref, logit_ref, ids_ref, keep_ref, cot_ref, up_ref, down_ref,
    attn_out, res_out, up_out, down_out, logit_out,
    qw, qsend, qrecv, pack_s, gw, gsend, grecv, agrad, asend, arecv,
    resid_s, cot_s, lg_s, ids_s, keep_s, cols, stage, probs, perm_s, bias_s,
    gswap, send_rows, recv_rows, rows_two, rows_all, w_all, pg_s, dots_s, part, xs, xr,
    ret_send, ret_recv, grads, zsend, zrecv,
    d_ss, d_rs, g_ss, g_rs, w_ss, w_rs, x_ss, x_rs, r_ss, r_rs, z_ss, z_rs, h_ss, h_rs, s_ss, s_rs,
):
    me_e = lax.axis_index("expert")
    me_s = lax.axis_index("space")
    mx = me_s // NZ
    mz = me_s % NZ
    zhi = me_e // 8
    x1 = mx + 1 - 2 * (mx % 2)
    x3 = NX - 1 - mx
    x2 = NX - 1 - x1
    me_yc = me_e % NYC
    mine = mx * (NX - 1 - mx) // 2
    other = 1 - mine
    zr = zhi * NZ + mz
    dev_x1 = x1 * NZ + mz
    dev_x3 = x3 * NZ + mz
    ring = []
    for step in (1, RING - 1):
        to = (zr + step) % RING
        ring.append(((to // NZ) * NYC + me_yc, mx * NZ + to % NZ))
    after = (me_s + 1) % (NX * NZ)
    before = (me_s + NX * NZ - 1) % (NX * NZ)

    def remote(src, dst, ss, rs, e, s):
        return pltpu.make_async_remote_copy(
            src_ref=src, dst_ref=dst, send_sem=ss, recv_sem=rs,
            device_id={"expert": e, "space": s}, device_id_type=pl.DeviceIdType.MESH,
        )

    barrier = pltpu.get_barrier_semaphore()

    def greet(e, s):
        pl.semaphore_signal(
            barrier, inc=1, device_id={"expert": e, "space": s}, device_id_type=pl.DeviceIdType.MESH
        )

    @pl.loop(1, NYC)
    def _(i):
        greet(zhi * NYC + (me_yc + i) % NYC, me_s)

    for e, s in ring:
        greet(e, s)
    for s in (dev_x1, dev_x3, after, before):
        greet(me_e, s)

    half_rows = WIN // 2
    qw[...] = jnp.zeros((2, 3, HALF, C), BF16)
    resid_s[...] = jnp.zeros((TOK, C), BF16)
    cot_s[...] = jnp.zeros((TOK, C), BF16)
    lg_s[...] = jnp.zeros((TOK, EXPERTS), F32)
    ids_s[...] = jnp.full((TOK, 2), -1, I32)
    keep_s[...] = jnp.zeros((TOK, 2), I32)
    for r in range(WIN):
        at = pl.ds(r * PADW, WIN)
        resid_s[at, :] = resid_ref[r]
        cot_s[at, :] = cot_ref[r]
        lg_s[at, :] = logit_ref[r]
        ids_s[at, :] = ids_ref[r]
        keep_s[at, :] = keep_ref[r]
    for r in range(half_rows):
        for k in range(3):
            qw[1, k, pl.ds(r * PADW, WIN), :] = attn_ref[k, r]
            qw[0, k, pl.ds(r * PADW, WIN), :] = attn_ref[k, half_rows + r]

    pl.semaphore_wait(barrier, NYC - 1 + 6)

    def weight_copy(way, step, m, j):
        chunk = (zr - step) % RING if way == 0 else (zr + step) % RING
        src = (up_ref, down_ref)[m].at[mine] if step == 0 and j == 0 else w_all.at[chunk, m, j]
        return remote(
            src, w_all.at[chunk, m, j], w_ss.at[way, step, m, j], w_rs.at[way, step, m, j], *ring[way]
        )

    def weight_arrived(way, step, m, j):
        chunk = (zr - 1 - step) % RING if way == 0 else (zr + 1 + step) % RING
        remote(
            w_all.at[chunk, m, j], w_all.at[chunk, m, j], w_ss.at[way, step, m, j],
            w_rs.at[way, step, m, j], *ring[way],
        ).wait_recv()

    pieces = [(m, j) for j in range(2) for m in range(2)]
    sent_w = []

    def start_weight(way, step, m, j):
        cp = weight_copy(way, step, m, j)
        cp.start()
        sent_w.append(cp)

    def forward_weights(step):
        for m, j in pieces:
            for way in range(2):
                weight_arrived(way, step - 1, m, j)
                if step < 3 or m == way:
                    start_weight(way, step, m, j)

    swap_w = [
        remote((up_ref, down_ref)[m].at[other], w_all.at[zr, m, 1], s_ss.at[m], s_rs.at[m], me_e, dev_x1)
        for m in range(2)
    ]
    for m in range(2):
        swap_w[m].start()
        for way in range(2):
            start_weight(way, 0, m, 0)

    def packing(count, dense):
        wide, narrow = count * HALF, dense
        i = iota((narrow, wide), 0)
        o = iota((narrow, wide), 1)
        keep_row = (o % PADW < WIN) & ((o // PADW) * WIN + o % PADW == i)
        return ones_where(keep_row)

    pack_s[...] = packing(3, 224)
    qsend[...] = dot(pack_s[...], qw[1].reshape(3 * HALF, C)).astype(BF16)
    halo_q = remote(qsend, qrecv, h_ss.at[0], h_rs.at[0], me_e, before)
    halo_q.start()

    resid = resid_s[...].astype(F32)
    rms = jnp.sqrt(jnp.mean(resid * resid, axis=-1, keepdims=True) + NORM_EPS)
    nf = resid / rms
    normed = nf.astype(BF16)
    cot = cot_s[...].astype(F32)
    lg = lg_s[...]
    ids = ids_s[...]
    keep = keep_s[...].astype(F32)
    id1, id2 = ids[:, 0:1], ids[:, 1:2]
    keep1, keep2 = keep[:, 0:1], keep[:, 1:2]
    expert = iota((TOK, EXPERTS), 1)
    oh1 = jnp.where(expert == id1, 1.0, 0.0)
    oh2 = jnp.where(expert == id2, 1.0, 0.0)
    l1 = jnp.sum(jnp.where(expert == id1, lg, 0.0), axis=-1, keepdims=True)
    l2 = jnp.sum(jnp.where(expert == id2, lg, 0.0), axis=-1, keepdims=True)
    lm = jnp.maximum(l1, l2)
    e1, e2 = jnp.exp(l1 - lm), jnp.exp(l2 - lm)
    gate1, gate2 = e1 / (e1 + e2), e2 / (e1 + e2)
    scaled1 = (gate1 * keep1 * cot).astype(BF16)
    scaled2 = (gate2 * keep2 * cot).astype(BF16)
    square_r, square_c = iota((TOK, TOK), 0), iota((TOK, TOK), 1)
    counts = dot(ones_where(square_c < square_r), (oh1 + oh2).astype(BF16))
    slot1 = jnp.sum(oh1 * counts, axis=-1, keepdims=True).astype(I32)
    slot2 = jnp.sum(oh2 * counts, axis=-1, keepdims=True).astype(I32)
    q1 = id1 * CAP + slot1
    q2 = id2 * CAP + slot2
    q1_row = jnp.sum(jnp.where(square_r == square_c, q1, 0), axis=0, keepdims=True)
    q2_row = jnp.sum(jnp.where(square_r == square_c, q2, 0), axis=0, keepdims=True)
    lane = iota((TOK, 128), 1)
    column = jnp.zeros((TOK, 128), F32)
    for i, v in enumerate((gate1, gate2, rms, keep1, keep2)):
        column = jnp.where(lane == i, v, column)
    cols[...] = column

    for m in range(2):
        swap_w[m].wait_recv()
        for way in range(2):
            start_weight(way, 0, m, 1)

    row = iota((TOK, 1), 0)
    src4 = ge(row, 48) + ge(row, 96) + ge(row, 144)
    rem = row - 48 * src4
    second = ge(rem, 24)

    @pl.loop(0, 2)
    def _(h):
        for p in range(2):
            q = (p * NYC + h * 4 + src4) * 24 + rem - 24 * second
            m1 = q == q1_row
            m2 = q == q2_row
            pn = ones_where((m1 | m2) & (second == 0))
            ps1 = ones_where(m1 & (second == 1))
            ps2 = ones_where(m2 & (second == 1))
            built = dot(pn, normed) + dot(ps1, scaled1) + dot(ps2, scaled2)
            send_rows[pl.ds(h * 4, 4), p] = built.astype(BF16).reshape(4, 48, C)
        for s in range(4):
            to = h * 4 + s

            @pl.when(to != me_yc)
            def _():
                remote(
                    send_rows.at[to], recv_rows.at[me_yc], d_ss.at[to], d_rs.at[me_yc],
                    zhi * NYC + to, me_s,
                ).start()

    recv_rows[me_yc] = send_rows[me_yc]

    b96 = ge(row, 96)
    o2 = row - 96 * b96
    b48 = ge(o2, 48)
    o3 = o2 - 48 * b48
    s12 = ge(o3, 12) + ge(o3, 24) + ge(o3, 36)
    perm_s[...] = ones_where(square_c == s12 * 48 + b48 * 24 + b96 * 12 + (o3 - 12 * s12))

    @pl.loop(0, 2)
    def _(g):
        for s in range(4):
            frm = g * 4 + s

            @pl.when(frm != me_yc)
            def _():
                remote(
                    send_rows.at[frm], recv_rows.at[frm], d_ss.at[frm], d_rs.at[frm],
                    zhi * NYC + frm, me_s,
                ).wait()

        for p in range(2):
            grp = 2 * p + g
            block = recv_rows[pl.ds(g * 4, 4), p].reshape(TOK, C)
            rows_two[grp] = dot(perm_s[...], block).astype(BF16).reshape(2, 2, 48, C)
            for which, j, dev in ((0, other, dev_x1), (1, mine, dev_x3)):
                remote(
                    rows_two.at[grp, j], rows_all.at[mx, grp], g_ss.at[which, grp],
                    g_rs.at[which, grp], me_e, dev,
                ).start()
            rows_all[mx, grp] = rows_two[grp, mine]

    forward_weights(1)
    w_all[zr, 0, 0] = up_ref[mine]
    w_all[zr, 1, 0] = down_ref[mine]

    pos_r = square_r % PADW
    pos_c = square_c % PADW
    differ = (pos_r >= half_rows) != (pos_c >= half_rows)
    is_last = me_s == NX * NZ - 1
    last_i = jnp.where(is_last, 1, 0)
    half_differ = (ge(square_r, HALF) != ge(square_c, HALF)) & ((square_r * 0 + last_i) == 1)
    bias = jnp.where(differ | half_differ, SCORE_MASK, 0.0)
    bias_s[...] = jnp.where(pos_c >= WIN, NO_KEY, bias)
    inv_sqrt = (C // HEADS) ** (-0.5)
    halo_q.wait_recv()
    qw[1] = dot_tn(pack_s[...], qrecv[...]).astype(BF16).reshape(3, HALF, C)

    head_lane = iota((1, 128), 1)

    def head_mask(h):
        return ones_where((head_lane >= h * 32) & (head_lane < (h + 1) * 32))

    @pl.loop(0, 4)
    def _(lg_i):
        lanes = pl.ds(pl.multiple_of(lg_i * 128, 128), 128)
        q = jnp.concatenate([qw[0, 0, :, lanes], qw[1, 0, :, lanes]], axis=0)
        k = jnp.concatenate([qw[0, 1, :, lanes], qw[1, 1, :, lanes]], axis=0)
        for h in range(4):
            sc = dot_nt(q * head_mask(h), k) * inv_sqrt + bias_s[...]
            ex = jnp.exp(sc - jnp.max(sc, axis=-1, keepdims=True))
            probs[lg_i * 4 + h] = ex / jnp.sum(ex, axis=-1, keepdims=True)

    def x_recv(which, grp):
        frm, dev = ((x1, dev_x1), (x3, dev_x3))[which]
        return remote(
            rows_all.at[frm, grp], rows_all.at[frm, grp], g_ss.at[which, grp], g_rs.at[which, grp],
            me_e, dev,
        )

    fwd_x = []

    def forward_rows(grp):
        x_recv(0, grp).wait_recv()
        cp = remote(
            rows_all.at[x1, grp], rows_all.at[x1, grp], g_ss.at[2, grp], g_rs.at[2, grp], me_e, dev_x3
        )
        cp.start()
        fwd_x.append(cp)

    forward_rows(0)
    forward_rows(2)
    forward_weights(2)
    forward_rows(1)
    forward_rows(3)
    for grp in range(4):
        x_recv(1, grp).wait_recv()
    for cp in fwd_x:
        cp.wait_recv()

    def rows_of(p, a):
        return rows_all[:, pl.ds(2 * p, 2), a].reshape(384, C)

    def slice_of(c, m):
        return jnp.concatenate([w_all[c, m, 0], w_all[c, m, 1]], axis=1)

    def expert_slice(c):
        p = c // NZ
        xn = rows_of(p, 0)
        xsc = rows_of(p, 1)
        pre = dot(xn, slice_of(c, 0))
        sq = pre * pre
        t = jnp.tanh(GELU_C * pre * (1.0 + GELU_A * sq))
        act = (0.5 * pre * (1.0 + t)).astype(BF16)
        slope = 0.5 * (1.0 + t) + 0.5 * GELU_C * pre * (1.0 - t * t) * (1.0 + 3.0 * GELU_A * sq)
        dact = dot(xsc, slice_of(c, 1))
        dots_s[c] = jnp.sum(act.astype(F32) * dact, axis=-1, keepdims=True)
        pg = (dact * slope).astype(BF16)
        pg_s[c] = pg
        grads[c, 0] = dot_tn(pg, xn).reshape(2, HID, C)
        grads[c, 1] = dot_tn(act, xsc).reshape(2, HID, C)

    def row_grads(p):
        pg = jnp.concatenate([pg_s[p * NZ + c] for c in range(NZ)], axis=1)
        up = jnp.concatenate([slice_of(p * NZ + c, 0) for c in range(NZ)], axis=1)
        part[:, pl.ds(2 * p, 2), pl.ds(0, 48), :] = dot_nt(pg, up).reshape(4, 2, 48, C)
        dsum = dots_s[p * NZ]
        for c in range(1, NZ):
            dsum = dsum + dots_s[p * NZ + c]
        hit = iota((48, C), 1) == iota((48, C), 0)
        for b in range(NX):
            for g in range(2):
                lo = (2 * b + g) * 48
                line = jnp.sum(jnp.where(hit, dsum[lo : lo + 48], 0.0), axis=0, keepdims=True)
                part[b, 2 * p + g, pl.ds(48, 16), :] = jnp.where(iota((16, C), 0) == 0, line, 0.0)

    def x_send(n, dev, slot, sem):
        return remote(xs.at[n], xr.at[slot], x_ss.at[n], x_rs.at[sem], me_e, dev)

    sent_z = []

    def start_sum(way, step, m, j, add):
        to = (zr + 4 - step) % RING if way == 0 else (zr + 4 + step) % RING
        value = grads[to, m, j]
        if add:
            cp = remote(
                zsend.at[way, step - 1, m, j], zrecv.at[way, step - 1, m, j],
                z_ss.at[way, step - 1, m, j], z_rs.at[way, step - 1, m, j], *ring[way],
            )
            cp.wait_recv()
            value = value + zrecv[way, step - 1, m, j].astype(F32)
        zsend[way, step, m, j] = value.astype(BF16)
        cp = remote(
            zsend.at[way, step, m, j], zrecv.at[way, step, m, j], z_ss.at[way, step, m, j],
            z_rs.at[way, step, m, j], *ring[way],
        )
        cp.start()
        sent_z.append(cp)

    def x_got(slot):
        return remote(xs.at[slot], xr.at[slot], x_ss.at[slot], x_rs.at[slot], me_e, dev_x1)

    sums = []
    def send_sum(slot, dev, value):
        xs[slot] = split_tail(value)
        sums.append(x_send(slot, dev, slot, slot))
        sums[-1].start()

    def away(n):
        return (zr + n + RING) % RING

    for n in (0, 1, -1):
        expert_slice(away(n))
    forward_weights(3)
    expert_slice(away(3))
    for j in (1, 0):
        start_sum(0, 1, 1, j, False)
    expert_slice(away(-3))
    for j in (1, 0):
        start_sum(1, 1, 0, j, False)
    expert_slice(away(2))
    expert_slice(away(-2))
    for way in range(2):
        for j in range(2):
            weight_arrived(way, 3, way, j)
    expert_slice(away(4))
    turn = [(m, j) for j in (1, 0) for m in range(2)]
    for m, j in turn:
        start_sum(m, 0, m, j, False)
    row_grads(1 - zhi)
    row_grads(zhi)
    for grp in range(4):
        send_sum(grp, dev_x3, part[x2, grp])
    for grp in range(4):
        send_sum(4 + grp, dev_x3, part[x3, grp])
    for m, j in turn:
        start_sum(m, 1, m, j, True)
    for grp in (0, 2, 1, 3):
        x_got(grp).wait_recv()
        send_sum(8 + grp, dev_x1, part[x1, grp] + xr[grp].astype(F32))

    ro = iota((128, 128), 0)
    rs = ge(ro, 32) + ge(ro, 64) + ge(ro, 96)
    rq = ro - 32 * rs
    rj = ge(rq, 12)
    half_of = jnp.where(rj == mine, 0, 64)
    want = half_of + rs * 12 + rq - 12 * rj
    want = jnp.where(rq < 24, want, jnp.where(rq < 26, rq + 24, jnp.where(rq < 28, rq + 86, -1)))
    back = ones_where(iota((128, 128), 1) == want)
    for g in range(2):
        for p in range(2):
            grp = 2 * p + g
            x_got(4 + grp).wait_recv()
            x_got(8 + grp).wait_recv()
            total = split_tail(part[mx, grp] + xr[4 + grp].astype(F32))
            both = jnp.concatenate([total, xr[8 + grp]], axis=0)
            ret_send[pl.ds(g * 4, 4), p] = dot(back, both).astype(BF16).reshape(4, 32, C)
        for s in range(4):
            to = g * 4 + s

            @pl.when(to != me_yc)
            def _():
                remote(
                    ret_send.at[to], ret_recv.at[me_yc], r_ss.at[to], r_rs.at[me_yc],
                    zhi * NYC + to, me_s,
                ).start()

    ret_recv[me_yc] = ret_send[me_yc]
    for m, j in turn:
        for way in range(2):
            start_sum(way, 2, m, j, True)

    @pl.loop(0, NYC)
    def _(frm):
        @pl.when(frm != me_yc)
        def _():
            remote(
                ret_send.at[frm], ret_recv.at[frm], r_ss.at[frm], r_rs.at[frm],
                zhi * NYC + frm, me_s,
            ).wait()

    returned = ret_recv[...].reshape(NE * 32, C)
    ids = ids_s[...]
    id1, id2 = ids[:, 0:1], ids[:, 1:2]
    expert = iota((TOK, EXPERTS), 1)
    hot1, hot2 = expert == id1, expert == id2
    oh1, oh2 = jnp.where(hot1, 1.0, 0.0), jnp.where(hot2, 1.0, 0.0)
    counts = dot(ones_where(square_c < square_r), (oh1 + oh2).astype(BF16))
    slot1 = jnp.sum(oh1 * counts, axis=-1, keepdims=True).astype(I32)
    slot2 = jnp.sum(oh2 * counts, axis=-1, keepdims=True).astype(I32)
    q1 = id1 * CAP + slot1
    q2 = id2 * CAP + slot2
    col = iota((TOK, NE * 32), 1)
    block_of = lax.shift_right_arithmetic(col, 5)
    pos = col - 32 * block_of
    dev = lax.shift_right_arithmetic(block_of, 1) + NYC * (block_of % 2)
    at = dev * 24 + pos
    pick = ones_where(((at == q1) | (at == q2)) & (pos < 24))
    norm_grad = dot(pick, returned)
    rms = cols[:, 2:3]
    resid = resid_s[...].astype(F32)
    nf = resid / rms
    inner = jnp.mean(norm_grad * nf, axis=-1, keepdims=True)
    cot = cot_s[...].astype(F32)
    res_grad = (cot + (norm_grad - nf * inner) / rms).astype(BF16)
    stage[...] = res_grad
    pack_one = packing(1, 80)
    gsend[...] = dot(pack_one, stage[pl.ds(0, HALF), :]).astype(BF16)
    halo_g = remote(gsend, grecv, h_ss.at[1], h_rs.at[1], me_e, before)
    halo_g.start()
    gw[0] = stage[pl.ds(HALF, HALF), :]
    for r in range(WIN):
        res_out[r] = stage[pl.ds(r * PADW, WIN), :]

    gate1, gate2 = cols[:, 0:1], cols[:, 1:2]
    keep1, keep2 = cols[:, 3:4], cols[:, 4:5]
    narrow = returned[:, :128]

    def gathered(idk, slotk):
        half = lax.shift_right_arithmetic(idk, 1)
        line = jnp.where(idk - 2 * half == mine, 24, 26)
        pickk = ones_where((dev == half) & ((pos == line) | (pos == line + 1)))
        found = dot(pickk, narrow)
        spot = (me_e % 4) * 12 + slotk
        return jnp.sum(jnp.where(iota((TOK, 128), 1) == spot, found, 0.0), axis=-1, keepdims=True)

    d1 = gathered(id1, slot1)
    d2 = gathered(id2, slot2)
    part1 = gate2 * d1 - gate1 * d2
    share = jnp.sum(oh1 * keep1 + oh2 * keep2, axis=0, keepdims=True) / (2.0 * WIN * WIN)
    lg = lg_s[...]
    lex = jnp.exp(lg - jnp.max(lg, axis=-1, keepdims=True))
    rp = lex / jnp.sum(lex, axis=-1, keepdims=True)
    share_mean = jnp.sum(rp * share, axis=-1, keepdims=True)
    lg_s[...] = (oh1 - oh2) * part1 + EXPERTS * rp * (share - share_mean)
    for r in range(WIN):
        logit_out[r] = lg_s[pl.ds(r * PADW, WIN), :]

    for m, j in turn:
        for way in range(2):
            start_sum(way, 3, m, j, True)

    halo_g.wait_recv()
    gw[1] = dot_tn(pack_one, grecv[...]).astype(BF16)

    @pl.loop(0, 4)
    def _(lg_i):
        lanes = pl.ds(pl.multiple_of(lg_i * 128, 128), 128)
        q = jnp.concatenate([qw[0, 0, :, lanes], qw[1, 0, :, lanes]], axis=0)
        k = jnp.concatenate([qw[0, 1, :, lanes], qw[1, 1, :, lanes]], axis=0)
        v = jnp.concatenate([qw[0, 2, :, lanes], qw[1, 2, :, lanes]], axis=0)
        gs = jnp.concatenate([gw[0, :, lanes], gw[1, :, lanes]], axis=0)
        dq = jnp.zeros((TOK, 128), F32)
        dk = jnp.zeros((TOK, 128), F32)
        dv = jnp.zeros((TOK, 128), F32)
        for h in range(4):
            hm = head_mask(h)
            gm = gs * hm
            pr = probs[lg_i * 4 + h]
            wt = pr.astype(BF16)
            pgrad = dot_nt(gm, v)
            delta = jnp.sum(wt.astype(F32) * pgrad, axis=-1, keepdims=True)
            sg = (pr * (pgrad - delta)).astype(BF16)
            dq = dq + dot(sg, k * hm)
            dk = dk + dot_tn(sg, q * hm)
            dv = dv + dot_tn(wt, gm)
        agrad[0, :, lanes] = (dq * inv_sqrt).astype(BF16)
        agrad[1, :, lanes] = (dk * inv_sqrt).astype(BF16)
        agrad[2, :, lanes] = dv.astype(BF16)

    asend[...] = dot(pack_s[...], agrad[:, pl.ds(HALF, HALF), :].reshape(3 * HALF, C)).astype(BF16)
    halo_a = remote(asend, arecv, h_ss.at[2], h_rs.at[2], me_e, after)
    halo_a.start()
    for r in range(half_rows):
        for k in range(3):
            attn_out[k, half_rows + r] = agrad[k, pl.ds(r * PADW, WIN), :]

    swap_g = []
    for j in (1, 0):
        for m, out in ((0, up_out), (1, down_out)):
            value = grads[zr, m, j]
            for way in range(2):
                remote(
                    zsend.at[way, 3, m, j], zrecv.at[way, 3, m, j], z_ss.at[way, 3, m, j],
                    z_rs.at[way, 3, m, j], *ring[way],
                ).wait_recv()
                value = value + zrecv[way, 3, m, j].astype(F32)
            if j == 1:
                gswap[0, m] = value.astype(BF16)
                cp = remote(gswap.at[0, m], gswap.at[1, m], s_ss.at[2 + m], s_rs.at[2 + m], me_e, dev_x1)
                cp.start()
                swap_g.append(cp)
            else:
                out[mine] = value.T
    for m, out in ((0, up_out), (1, down_out)):
        swap_g[m].wait_recv()
        out[other] = gswap[1, m].astype(F32).T

    halo_a.wait_recv()
    qw[1] = dot_tn(pack_s[...], arecv[...]).astype(BF16).reshape(3, HALF, C)
    for r in range(half_rows):
        for k in range(3):
            attn_out[k, r] = qw[1, k, pl.ds(r * PADW, WIN), :]

    for cp in (*sent_w, *swap_w, *fwd_x, *sums, *sent_z, *swap_g, halo_q, halo_g, halo_a):
        cp.wait_send()
    for grp in range(4):
        for which in range(2):
            x_recv(which, grp).wait_send()


def per_device(attn_inputs, residual, logits, expert_ids, keep_mask, cotangent, up_weight, down_weight):
    vmem = pl.BlockSpec(memory_space=pltpu.VMEM)
    dma = pltpu.SemaphoreType.DMA
    outs = pl.pallas_call(
        kernel,
        out_shape=(
            jax.ShapeDtypeStruct((3, WIN, WIN, C), BF16),
            jax.ShapeDtypeStruct((WIN, WIN, C), BF16),
            jax.ShapeDtypeStruct((2, C, HID), F32),
            jax.ShapeDtypeStruct((2, C, HID), F32),
            jax.ShapeDtypeStruct((WIN, WIN, EXPERTS), F32),
        ),
        in_specs=[vmem] * 8,
        out_specs=(vmem,) * 5,
        scratch_shapes=[
            pltpu.VMEM((2, 3, HALF, C), BF16),
            pltpu.VMEM((224, C), BF16),
            pltpu.VMEM((224, C), BF16),
            pltpu.VMEM((224, 3 * HALF), BF16),
            pltpu.VMEM((2, HALF, C), BF16),
            pltpu.VMEM((80, C), BF16),
            pltpu.VMEM((80, C), BF16),
            pltpu.VMEM((3, TOK, C), BF16),
            pltpu.VMEM((224, C), BF16),
            pltpu.VMEM((224, C), BF16),
            pltpu.VMEM((TOK, C), BF16),
            pltpu.VMEM((TOK, C), BF16),
            pltpu.VMEM((TOK, EXPERTS), F32),
            pltpu.VMEM((TOK, 2), I32),
            pltpu.VMEM((TOK, 2), I32),
            pltpu.VMEM((TOK, 128), F32),
            pltpu.VMEM((TOK, C), BF16),
            pltpu.VMEM((HEADS, TOK, TOK), F32),
            pltpu.VMEM((TOK, TOK), BF16),
            pltpu.VMEM((TOK, TOK), F32),
            pltpu.VMEM((2, 2, HID, C), BF16),
            pltpu.VMEM((NYC, 2, 48, C), BF16),
            pltpu.VMEM((NYC, 2, 48, C), BF16),
            pltpu.VMEM((4, 2, 2, 48, C), BF16),
            pltpu.VMEM((NX, 4, 2, 48, C), BF16),
            pltpu.VMEM((RING, 2, 2, C, HID), BF16),
            pltpu.VMEM((RING, 384, 2 * HID), BF16),
            pltpu.VMEM((RING, 384, 1), F32),
            pltpu.VMEM((NX, 4, 64, C), F32),
            pltpu.VMEM((12, 64, C), BF16),
            pltpu.VMEM((12, 64, C), BF16),
            pltpu.VMEM((NYC, 2, 32, C), BF16),
            pltpu.VMEM((NYC, 2, 32, C), BF16),
            pltpu.VMEM((RING, 2, 2, HID, C), F32),
            pltpu.VMEM((2, 4, 2, 2, HID, C), BF16),
            pltpu.VMEM((2, 4, 2, 2, HID, C), BF16),
            dma((NYC,)), dma((NYC,)),
            dma((3, 4)), dma((3, 4)),
            dma((2, 4, 2, 2)), dma((2, 4, 2, 2)),
            dma((12,)), dma((12,)),
            dma((NYC,)), dma((NYC,)),
            dma((2, 4, 2, 2)), dma((2, 4, 2, 2)),
            dma((3,)), dma((3,)),
            dma((4,)), dma((4,)),
        ],
        compiler_params=pltpu.CompilerParams(
            collective_id=0, has_side_effects=True, vmem_limit_bytes=56 * 1024 * 1024
        ),
    )(
        attn_inputs[:, 0], residual[0], logits[0], expert_ids[0], keep_mask[0], cotangent[0],
        up_weight, down_weight,
    )
    attn_grad, res_grad, up_grad, down_grad, logit_grad = outs
    return attn_grad[:, None], res_grad[None], up_grad, down_grad, logit_grad[None]


def solution(mesh):
    in_specs = (
        P(None, "expert", "space", None, None),
        P("expert", "space", None, None),
        P("expert", "space", None, None),
        P("expert", "space", None, None),
        P("expert", "space", None, None),
        P("expert", "space", None, None),
        P("expert", None, "space"),
        P("expert", None, "space"),
    )
    out_specs = (
        P(None, "expert", "space", None, None),
        P("expert", "space", None, None),
        P("expert", None, "space"),
        P("expert", None, "space"),
        P("expert", "space", None, None),
    )
    return jax.shard_map(
        per_device, mesh=mesh, in_specs=in_specs, out_specs=out_specs, check_vma=False
    )
```

```python
import jax
import jax.numpy as jnp
from jax import lax
from jax.experimental import pallas as pl
from jax.experimental.pallas import tpu as pltpu
from jax.sharding import PartitionSpec as P

WIN = 12
PADW = 16
TOK = WIN * PADW
HALF = TOK // 2
C = 512
HEADS = 16
EXPERTS = 32
CAP = 12
NE = 16
NX = 4
NZ = 4
RING = 8
NYC = 8
HID = 128
NORM_EPS = 1e-06
SCORE_MASK = -100.0
NO_KEY = -1e30
GELU_C = 0.7978845608028654
GELU_A = 0.044715
F32 = jnp.float32
BF16 = jnp.bfloat16
I32 = jnp.int32


def iota(shape, dim):
    return lax.broadcasted_iota(I32, shape, dim)


def dot(a, b):
    return lax.dot_general(a, b, (((1,), (0,)), ((), ())), preferred_element_type=F32)


def dot_nt(a, b):
    return lax.dot_general(a, b, (((1,), (1,)), ((), ())), preferred_element_type=F32)


def dot_tn(a, b):
    return lax.dot_general(a, b, (((0,), (0,)), ((), ())), preferred_element_type=F32)


def ge(a, n):
    return (a >= n).astype(I32)


def ones_where(cond):
    return jnp.where(cond, 1.0, 0.0).astype(BF16)


def split_tail(x):
    total = x[48:49] + x[49:50]
    high = total.astype(BF16).astype(F32)
    low = total - high
    row = iota((16, C), 0)
    tail = jnp.where(row == 0, high, jnp.where(row == 1, low, 0.0))
    return jnp.concatenate([x[:48], tail], axis=0).astype(BF16)


def kernel(
    attn_ref, resid_ref, logit_ref, ids_ref, keep_ref, cot_ref, up_ref, down_ref,
    attn_out, res_out, up_out, down_out, logit_out,
    qw, qsend, qrecv, pack_s, gw, gsend, grecv, agrad, asend, arecv,
    resid_s, cot_s, lg_s, ids_s, keep_s, cols, stage, probs, perm_s, bias_s,
    gswap, send_rows, recv_rows, rows_two, rows_all, w_all, pg_s, dots_s, part, xs, xr,
    ret_send, ret_recv, grads, zsend, zrecv,
    d_ss, d_rs, g_ss, g_rs, w_ss, w_rs, x_ss, x_rs, r_ss, r_rs, z_ss, z_rs, h_ss, h_rs, s_ss, s_rs,
):
    me_e = lax.axis_index("expert")
    me_s = lax.axis_index("space")
    mx = me_s // NZ
    mz = me_s % NZ
    zhi = me_e // 8
    x1 = mx + 1 - 2 * (mx % 2)
    x3 = NX - 1 - mx
    x2 = NX - 1 - x1
    me_yc = me_e % NYC
    mine = mx * (NX - 1 - mx) // 2
    other = 1 - mine
    zr = zhi * NZ + mz
    dev_x1 = x1 * NZ + mz
    dev_x3 = x3 * NZ + mz
    ring = []
    for step in (1, RING - 1):
        to = (zr + step) % RING
        ring.append(((to // NZ) * NYC + me_yc, mx * NZ + to % NZ))
    after = (me_s + 1) % (NX * NZ)
    before = (me_s + NX * NZ - 1) % (NX * NZ)

    def remote(src, dst, ss, rs, e, s):
        return pltpu.make_async_remote_copy(
            src_ref=src, dst_ref=dst, send_sem=ss, recv_sem=rs,
            device_id={"expert": e, "space": s}, device_id_type=pl.DeviceIdType.MESH,
        )

    barrier = pltpu.get_barrier_semaphore()

    def greet(e, s):
        pl.semaphore_signal(
            barrier, inc=1, device_id={"expert": e, "space": s}, device_id_type=pl.DeviceIdType.MESH
        )

    @pl.loop(1, NYC)
    def _(i):
        greet(zhi * NYC + (me_yc + i) % NYC, me_s)

    for e, s in ring:
        greet(e, s)
    for s in (dev_x1, dev_x3, after, before):
        greet(me_e, s)

    pl.semaphore_wait(barrier, NYC - 1 + 6)

    def weight_copy(way, step, m, j):
        chunk = (zr - step) % RING if way == 0 else (zr + step) % RING
        src = (up_ref, down_ref)[m].at[mine] if step == 0 and j == 0 else w_all.at[chunk, m, j]
        return remote(
            src, w_all.at[chunk, m, j], w_ss.at[way, step, m, j], w_rs.at[way, step, m, j], *ring[way]
        )

    def weight_arrived(way, step, m, j):
        chunk = (zr - 1 - step) % RING if way == 0 else (zr + 1 + step) % RING
        remote(
            w_all.at[chunk, m, j], w_all.at[chunk, m, j], w_ss.at[way, step, m, j],
            w_rs.at[way, step, m, j], *ring[way],
        ).wait_recv()

    pieces = [(m, j) for j in range(2) for m in range(2)]
    sent_w = []

    def start_weight(way, step, m, j):
        cp = weight_copy(way, step, m, j)
        cp.start()
        sent_w.append(cp)

    def forward_weights(step, j):
        for m in range(2):
            for way in range(2):
                weight_arrived(way, step - 1, m, j)
                if step < 3 or m == way:
                    start_weight(way, step, m, j)

    swap_w = [
        remote((up_ref, down_ref)[m].at[other], w_all.at[zr, m, 1], s_ss.at[m], s_rs.at[m], me_e, dev_x1)
        for m in range(2)
    ]
    for m in range(2):
        swap_w[m].start()
        for way in range(2):
            start_weight(way, 0, m, 0)

    half_rows = WIN // 2
    qw[...] = jnp.zeros((2, 3, HALF, C), BF16)
    resid_s[...] = jnp.zeros((TOK, C), BF16)
    cot_s[...] = jnp.zeros((TOK, C), BF16)
    lg_s[...] = jnp.zeros((TOK, EXPERTS), F32)
    ids_s[...] = jnp.full((TOK, 2), -1, I32)
    keep_s[...] = jnp.zeros((TOK, 2), I32)
    for r in range(WIN):
        at = pl.ds(r * PADW, WIN)
        resid_s[at, :] = resid_ref[r]
        cot_s[at, :] = cot_ref[r]
        lg_s[at, :] = logit_ref[pl.ds(r * WIN, WIN), 0, :]
        for ref, to in ((ids_ref, ids_s), (keep_ref, keep_s)):
            for k in range(2):
                line = ref[r, pl.ds(k, 1), :]
                to[at, pl.ds(k, 1)] = jnp.sum(
                    jnp.where(iota((WIN, WIN), 0) == iota((WIN, WIN), 1), line, 0), axis=1, keepdims=True
                )
    for r in range(half_rows):
        for k in range(3):
            qw[1, k, pl.ds(r * PADW, WIN), :] = attn_ref[k, r]
            qw[0, k, pl.ds(r * PADW, WIN), :] = attn_ref[k, half_rows + r]

    def packing(count, dense):
        wide, narrow = count * HALF, dense
        i = iota((narrow, wide), 0)
        o = iota((narrow, wide), 1)
        keep_row = (o % PADW < WIN) & ((o // PADW) * WIN + o % PADW == i)
        return ones_where(keep_row)

    pack_s[...] = packing(3, 224)
    qsend[...] = dot(pack_s[...], qw[1].reshape(3 * HALF, C)).astype(BF16)
    halo_q = remote(qsend, qrecv, h_ss.at[0], h_rs.at[0], me_e, before)
    halo_q.start()

    resid = resid_s[...].astype(F32)
    rms = jnp.sqrt(jnp.mean(resid * resid, axis=-1, keepdims=True) + NORM_EPS)
    nf = resid / rms
    normed = nf.astype(BF16)
    cot = cot_s[...].astype(F32)
    lg = lg_s[...]
    ids = ids_s[...]
    keep = keep_s[...].astype(F32)
    id1, id2 = ids[:, 0:1], ids[:, 1:2]
    keep1, keep2 = keep[:, 0:1], keep[:, 1:2]
    expert = iota((TOK, EXPERTS), 1)
    oh1 = jnp.where(expert == id1, 1.0, 0.0)
    oh2 = jnp.where(expert == id2, 1.0, 0.0)
    l1 = jnp.sum(jnp.where(expert == id1, lg, 0.0), axis=-1, keepdims=True)
    l2 = jnp.sum(jnp.where(expert == id2, lg, 0.0), axis=-1, keepdims=True)
    lm = jnp.maximum(l1, l2)
    e1, e2 = jnp.exp(l1 - lm), jnp.exp(l2 - lm)
    gate1, gate2 = e1 / (e1 + e2), e2 / (e1 + e2)
    scaled1 = (gate1 * keep1 * cot).astype(BF16)
    scaled2 = (gate2 * keep2 * cot).astype(BF16)
    square_r, square_c = iota((TOK, TOK), 0), iota((TOK, TOK), 1)
    counts = dot(ones_where(square_c < square_r), (oh1 + oh2).astype(BF16))
    slot1 = jnp.sum(oh1 * counts, axis=-1, keepdims=True).astype(I32)
    slot2 = jnp.sum(oh2 * counts, axis=-1, keepdims=True).astype(I32)
    q1 = id1 * CAP + slot1
    q2 = id2 * CAP + slot2
    q1_row = jnp.sum(jnp.where(square_r == square_c, q1, 0), axis=0, keepdims=True)
    q2_row = jnp.sum(jnp.where(square_r == square_c, q2, 0), axis=0, keepdims=True)
    lane = iota((TOK, 128), 1)
    column = jnp.zeros((TOK, 128), F32)
    for i, v in enumerate((gate1, gate2, rms, keep1, keep2)):
        column = jnp.where(lane == i, v, column)
    cols[...] = column

    row = iota((TOK, 1), 0)
    src4 = ge(row, 48) + ge(row, 96) + ge(row, 144)
    rem = row - 48 * src4
    second = ge(rem, 24)

    @pl.loop(0, 2)
    def _(h):
        for p in range(2):
            q = (p * NYC + h * 4 + src4) * 24 + rem - 24 * second
            m1 = q == q1_row
            m2 = q == q2_row
            pn = ones_where((m1 | m2) & (second == 0))
            ps1 = ones_where(m1 & (second == 1))
            ps2 = ones_where(m2 & (second == 1))
            built = dot(pn, normed) + dot(ps1, scaled1) + dot(ps2, scaled2)
            send_rows[pl.ds(h * 4, 4), p] = built.astype(BF16).reshape(4, 48, C)
        for s in range(4):
            to = h * 4 + s

            @pl.when(to != me_yc)
            def _():
                remote(
                    send_rows.at[to], recv_rows.at[me_yc], d_ss.at[to], d_rs.at[me_yc],
                    zhi * NYC + to, me_s,
                ).start()

    recv_rows[me_yc] = send_rows[me_yc]
    for m in range(2):
        swap_w[m].wait_recv()
        for way in range(2):
            start_weight(way, 0, m, 1)

    b96 = ge(row, 96)
    o2 = row - 96 * b96
    b48 = ge(o2, 48)
    o3 = o2 - 48 * b48
    s12 = ge(o3, 12) + ge(o3, 24) + ge(o3, 36)
    perm_s[...] = ones_where(square_c == s12 * 48 + b48 * 24 + b96 * 12 + (o3 - 12 * s12))

    forward_weights(1, 0)

    @pl.loop(0, 2)
    def _(g):
        for s in range(4):
            frm = g * 4 + s

            @pl.when(frm != me_yc)
            def _():
                remote(
                    send_rows.at[frm], recv_rows.at[frm], d_ss.at[frm], d_rs.at[frm],
                    zhi * NYC + frm, me_s,
                ).wait()

        for p in range(2):
            grp = 2 * p + g
            block = recv_rows[pl.ds(g * 4, 4), p].reshape(TOK, C)
            rows_two[grp] = dot(perm_s[...], block).astype(BF16).reshape(2, 2, 48, C)
            for which, j, dev in ((0, other, dev_x1), (1, mine, dev_x3)):
                remote(
                    rows_two.at[grp, j], rows_all.at[mx, grp], g_ss.at[which, grp],
                    g_rs.at[which, grp], me_e, dev,
                ).start()
            rows_all[mx, grp] = rows_two[grp, mine]

    forward_weights(1, 1)
    w_all[zr, 0, 0] = up_ref[mine]
    w_all[zr, 1, 0] = down_ref[mine]

    pos_r = square_r % PADW
    pos_c = square_c % PADW
    differ = (pos_r >= half_rows) != (pos_c >= half_rows)
    is_last = me_s == NX * NZ - 1
    last_i = jnp.where(is_last, 1, 0)
    half_differ = (ge(square_r, HALF) != ge(square_c, HALF)) & ((square_r * 0 + last_i) == 1)
    bias = jnp.where(differ | half_differ, SCORE_MASK, 0.0)
    bias_s[...] = jnp.where(pos_c >= WIN, NO_KEY, bias)
    inv_sqrt = (C // HEADS) ** (-0.5)
    halo_q.wait_recv()
    qw[1] = dot_tn(pack_s[...], qrecv[...]).astype(BF16).reshape(3, HALF, C)

    head_lane = iota((1, 128), 1)

    def head_mask(h):
        return ones_where((head_lane >= h * 32) & (head_lane < (h + 1) * 32))

    @pl.loop(0, 4)
    def _(lg_i):
        lanes = pl.ds(pl.multiple_of(lg_i * 128, 128), 128)
        q = jnp.concatenate([qw[0, 0, :, lanes], qw[1, 0, :, lanes]], axis=0)
        k = jnp.concatenate([qw[0, 1, :, lanes], qw[1, 1, :, lanes]], axis=0)
        for h in range(4):
            sc = dot_nt(q * head_mask(h), k) * inv_sqrt + bias_s[...]
            ex = jnp.exp(sc - jnp.max(sc, axis=-1, keepdims=True))
            probs[lg_i * 4 + h] = ex / jnp.sum(ex, axis=-1, keepdims=True)

    def x_recv(which, grp):
        frm, dev = ((x1, dev_x1), (x3, dev_x3))[which]
        return remote(
            rows_all.at[frm, grp], rows_all.at[frm, grp], g_ss.at[which, grp], g_rs.at[which, grp],
            me_e, dev,
        )

    fwd_x = []

    def forward_rows(grp):
        x_recv(0, grp).wait_recv()
        cp = remote(
            rows_all.at[x1, grp], rows_all.at[x1, grp], g_ss.at[2, grp], g_rs.at[2, grp], me_e, dev_x3
        )
        cp.start()
        fwd_x.append(cp)

    forward_rows(0)
    forward_rows(2)
    forward_weights(2, 0)
    forward_rows(1)
    forward_rows(3)
    forward_weights(2, 1)
    forward_weights(3, 0)
    forward_weights(3, 1)
    for grp in range(4):
        x_recv(1, grp).wait_recv()
    for cp in fwd_x:
        cp.wait_recv()

    def rows_of(p, a):
        return rows_all[:, pl.ds(2 * p, 2), a].reshape(384, C)

    def slice_of(c, m):
        return jnp.concatenate([w_all[c, m, 0], w_all[c, m, 1]], axis=1)

    def expert_slice(c):
        p = c // NZ
        xn = rows_of(p, 0)
        xsc = rows_of(p, 1)
        pre = dot(xn, slice_of(c, 0))
        sq = pre * pre
        t = jnp.tanh(GELU_C * pre * (1.0 + GELU_A * sq))
        act = (0.5 * pre * (1.0 + t)).astype(BF16)
        slope = 0.5 * (1.0 + t) + 0.5 * GELU_C * pre * (1.0 - t * t) * (1.0 + 3.0 * GELU_A * sq)
        dact = dot(xsc, slice_of(c, 1))
        dots_s[c] = jnp.sum(act.astype(F32) * dact, axis=-1, keepdims=True)
        pg = (dact * slope).astype(BF16)
        pg_s[c] = pg
        grads[c, 0] = dot_tn(pg, xn).reshape(2, HID, C)
        grads[c, 1] = dot_tn(act, xsc).reshape(2, HID, C)

    def row_grads(p):
        pg = jnp.concatenate([pg_s[p * NZ + c] for c in range(NZ)], axis=1)
        up = jnp.concatenate([slice_of(p * NZ + c, 0) for c in range(NZ)], axis=1)
        part[:, pl.ds(2 * p, 2), pl.ds(0, 48), :] = dot_nt(pg, up).reshape(4, 2, 48, C)
        dsum = dots_s[p * NZ]
        for c in range(1, NZ):
            dsum = dsum + dots_s[p * NZ + c]
        hit = iota((48, C), 1) == iota((48, C), 0)
        for b in range(NX):
            for g in range(2):
                lo = (2 * b + g) * 48
                line = jnp.sum(jnp.where(hit, dsum[lo : lo + 48], 0.0), axis=0, keepdims=True)
                part[b, 2 * p + g, pl.ds(48, 16), :] = jnp.where(iota((16, C), 0) == 0, line, 0.0)

    def x_send(n, dev, slot, sem):
        return remote(xs.at[n], xr.at[slot], x_ss.at[n], x_rs.at[sem], me_e, dev)

    sent_z = []

    def start_sum(way, step, m, j, add):
        to = (zr + 4 - step) % RING if way == 0 else (zr + 4 + step) % RING
        value = grads[to, m, j]
        if add:
            cp = remote(
                zsend.at[way, step - 1, m, j], zrecv.at[way, step - 1, m, j],
                z_ss.at[way, step - 1, m, j], z_rs.at[way, step - 1, m, j], *ring[way],
            )
            cp.wait_recv()
            value = value + zrecv[way, step - 1, m, j].astype(F32)
        zsend[way, step, m, j] = value.astype(BF16)
        cp = remote(
            zsend.at[way, step, m, j], zrecv.at[way, step, m, j], z_ss.at[way, step, m, j],
            z_rs.at[way, step, m, j], *ring[way],
        )
        cp.start()
        sent_z.append(cp)

    def x_got(slot):
        return remote(xs.at[slot], xr.at[slot], x_ss.at[slot], x_rs.at[slot], me_e, dev_x1)

    sums = []
    def send_sum(slot, dev, value):
        xs[slot] = split_tail(value)
        sums.append(x_send(slot, dev, slot, slot))
        sums[-1].start()

    def away(n):
        return (zr + n + RING) % RING

    expert_slice(away(3))
    for j in (1, 0):
        start_sum(0, 1, 1, j, False)
    expert_slice(away(-3))
    for j in (1, 0):
        start_sum(1, 1, 0, j, False)
    for n in (0, 1, -1, 2, -2):
        expert_slice(away(n))
    row_grads(zhi)
    for g in range(2):
        send_sum(2 * zhi + g, dev_x3, part[x2, 2 * zhi + g])
    for g in range(2):
        send_sum(4 + 2 * zhi + g, dev_x3, part[x3, 2 * zhi + g])
    for way in range(2):
        for j in range(2):
            weight_arrived(way, 3, way, j)
    expert_slice(away(4))
    turn = [(m, j) for j in (1, 0) for m in range(2)]
    for m, j in turn:
        start_sum(m, 0, m, j, False)
    far = 1 - zhi
    row_grads(far)
    for g in range(2):
        send_sum(2 * far + g, dev_x3, part[x2, 2 * far + g])
    for g in range(2):
        send_sum(4 + 2 * far + g, dev_x3, part[x3, 2 * far + g])

    def relay(grp):
        x_got(grp).wait_recv()
        send_sum(8 + grp, dev_x1, part[x1, grp] + xr[grp].astype(F32))

    for g in range(2):
        relay(2 * zhi + g)
    for m, j in turn:
        start_sum(m, 1, m, j, True)
    for g in range(2):
        relay(2 * far + g)
    for j in (1, 0):
        for way in range(2):
            start_sum(way, 2, 1 - way, j, True)

    ro = iota((128, 128), 0)
    rs = ge(ro, 32) + ge(ro, 64) + ge(ro, 96)
    rq = ro - 32 * rs
    rj = ge(rq, 12)
    half_of = jnp.where(rj == mine, 0, 64)
    want = half_of + rs * 12 + rq - 12 * rj
    want = jnp.where(rq < 24, want, jnp.where(rq < 26, rq + 24, jnp.where(rq < 28, rq + 86, -1)))
    back = ones_where(iota((128, 128), 1) == want)
    for g in range(2):
        for p in range(2):
            grp = 2 * p + g
            x_got(4 + grp).wait_recv()
            x_got(8 + grp).wait_recv()
            total = split_tail(part[mx, grp] + xr[4 + grp].astype(F32))
            both = jnp.concatenate([total, xr[8 + grp]], axis=0)
            ret_send[pl.ds(g * 4, 4), p] = dot(back, both).astype(BF16).reshape(4, 32, C)
        for s in range(4):
            to = g * 4 + s

            @pl.when(to != me_yc)
            def _():
                remote(
                    ret_send.at[to], ret_recv.at[me_yc], r_ss.at[to], r_rs.at[me_yc],
                    zhi * NYC + to, me_s,
                ).start()

    ret_recv[me_yc] = ret_send[me_yc]
    for j in (1, 0):
        for way in range(2):
            start_sum(way, 2, way, j, True)

    @pl.loop(0, NYC)
    def _(frm):
        @pl.when(frm != me_yc)
        def _():
            remote(
                ret_send.at[frm], ret_recv.at[frm], r_ss.at[frm], r_rs.at[frm],
                zhi * NYC + frm, me_s,
            ).wait()

    for j in (1, 0):
        for way in range(2):
            start_sum(way, 3, 1 - way, j, True)

    returned = ret_recv[...].reshape(NE * 32, C)
    ids = ids_s[...]
    id1, id2 = ids[:, 0:1], ids[:, 1:2]
    expert = iota((TOK, EXPERTS), 1)
    hot1, hot2 = expert == id1, expert == id2
    oh1, oh2 = jnp.where(hot1, 1.0, 0.0), jnp.where(hot2, 1.0, 0.0)
    counts = dot(ones_where(square_c < square_r), (oh1 + oh2).astype(BF16))
    slot1 = jnp.sum(oh1 * counts, axis=-1, keepdims=True).astype(I32)
    slot2 = jnp.sum(oh2 * counts, axis=-1, keepdims=True).astype(I32)
    q1 = id1 * CAP + slot1
    q2 = id2 * CAP + slot2
    col = iota((TOK, NE * 32), 1)
    block_of = lax.shift_right_arithmetic(col, 5)
    pos = col - 32 * block_of
    dev = lax.shift_right_arithmetic(block_of, 1) + NYC * (block_of % 2)
    at = dev * 24 + pos
    pick = ones_where(((at == q1) | (at == q2)) & (pos < 24))
    norm_grad = dot(pick, returned)
    rms = cols[:, 2:3]
    resid = resid_s[...].astype(F32)
    nf = resid / rms
    inner = jnp.mean(norm_grad * nf, axis=-1, keepdims=True)
    cot = cot_s[...].astype(F32)
    res_grad = (cot + (norm_grad - nf * inner) / rms).astype(BF16)
    stage[...] = res_grad
    pack_one = packing(1, 80)
    gsend[...] = dot(pack_one, stage[pl.ds(0, HALF), :]).astype(BF16)
    halo_g = remote(gsend, grecv, h_ss.at[1], h_rs.at[1], me_e, before)
    halo_g.start()
    gw[0] = stage[pl.ds(HALF, HALF), :]
    for r in range(WIN):
        res_out[r] = stage[pl.ds(r * PADW, WIN), :]

    gate1, gate2 = cols[:, 0:1], cols[:, 1:2]
    keep1, keep2 = cols[:, 3:4], cols[:, 4:5]
    narrow = returned[:, :128]

    def gathered(idk, slotk):
        half = lax.shift_right_arithmetic(idk, 1)
        line = jnp.where(idk - 2 * half == mine, 24, 26)
        pickk = ones_where((dev == half) & ((pos == line) | (pos == line + 1)))
        found = dot(pickk, narrow)
        spot = (me_e % 4) * 12 + slotk
        return jnp.sum(jnp.where(iota((TOK, 128), 1) == spot, found, 0.0), axis=-1, keepdims=True)

    d1 = gathered(id1, slot1)
    d2 = gathered(id2, slot2)
    part1 = gate2 * d1 - gate1 * d2
    share = jnp.sum(oh1 * keep1 + oh2 * keep2, axis=0, keepdims=True) / (2.0 * WIN * WIN)
    lg = lg_s[...]
    lex = jnp.exp(lg - jnp.max(lg, axis=-1, keepdims=True))
    rp = lex / jnp.sum(lex, axis=-1, keepdims=True)
    share_mean = jnp.sum(rp * share, axis=-1, keepdims=True)
    lg_s[...] = (oh1 - oh2) * part1 + EXPERTS * rp * (share - share_mean)
    for r in range(WIN):
        logit_out[pl.ds(r * WIN, WIN), 0, :] = lg_s[pl.ds(r * PADW, WIN), :]

    for j in (1, 0):
        for way in range(2):
            start_sum(way, 3, way, j, True)

    halo_g.wait_recv()
    gw[1] = dot_tn(pack_one, grecv[...]).astype(BF16)

    @pl.loop(0, 4)
    def _(lg_i):
        lanes = pl.ds(pl.multiple_of(lg_i * 128, 128), 128)
        q = jnp.concatenate([qw[0, 0, :, lanes], qw[1, 0, :, lanes]], axis=0)
        k = jnp.concatenate([qw[0, 1, :, lanes], qw[1, 1, :, lanes]], axis=0)
        v = jnp.concatenate([qw[0, 2, :, lanes], qw[1, 2, :, lanes]], axis=0)
        gs = jnp.concatenate([gw[0, :, lanes], gw[1, :, lanes]], axis=0)
        dq = jnp.zeros((TOK, 128), F32)
        dk = jnp.zeros((TOK, 128), F32)
        dv = jnp.zeros((TOK, 128), F32)
        for h in range(4):
            hm = head_mask(h)
            gm = gs * hm
            pr = probs[lg_i * 4 + h]
            wt = pr.astype(BF16)
            pgrad = dot_nt(gm, v)
            delta = jnp.sum(wt.astype(F32) * pgrad, axis=-1, keepdims=True)
            sg = (pr * (pgrad - delta)).astype(BF16)
            dq = dq + dot(sg, k * hm)
            dk = dk + dot_tn(sg, q * hm)
            dv = dv + dot_tn(wt, gm)
        agrad[0, :, lanes] = (dq * inv_sqrt).astype(BF16)
        agrad[1, :, lanes] = (dk * inv_sqrt).astype(BF16)
        agrad[2, :, lanes] = dv.astype(BF16)

    asend[...] = dot(pack_s[...], agrad[:, pl.ds(HALF, HALF), :].reshape(3 * HALF, C)).astype(BF16)
    halo_a = remote(asend, arecv, h_ss.at[2], h_rs.at[2], me_e, after)
    halo_a.start()
    for r in range(half_rows):
        for k in range(3):
            attn_out[k, half_rows + r] = agrad[k, pl.ds(r * PADW, WIN), :]

    swap_g = []
    for j in (1, 0):
        for m, out in ((0, up_out), (1, down_out)):
            value = grads[zr, m, j]
            for way in range(2):
                remote(
                    zsend.at[way, 3, m, j], zrecv.at[way, 3, m, j], z_ss.at[way, 3, m, j],
                    z_rs.at[way, 3, m, j], *ring[way],
                ).wait_recv()
                value = value + zrecv[way, 3, m, j].astype(F32)
            if j == 1:
                gswap[0, m] = value.astype(BF16)
                cp = remote(gswap.at[0, m], gswap.at[1, m], s_ss.at[2 + m], s_rs.at[2 + m], me_e, dev_x1)
                cp.start()
                swap_g.append(cp)
            else:
                out[mine] = value.T
    for m, out in ((0, up_out), (1, down_out)):
        swap_g[m].wait_recv()
        out[other] = gswap[1, m].astype(F32).T

    halo_a.wait_recv()
    qw[1] = dot_tn(pack_s[...], arecv[...]).astype(BF16).reshape(3, HALF, C)
    for r in range(half_rows):
        for k in range(3):
            attn_out[k, r] = qw[1, k, pl.ds(r * PADW, WIN), :]

    for cp in (*sent_w, *swap_w, *fwd_x, *sums, *sent_z, *swap_g, halo_q, halo_g, halo_a):
        cp.wait_send()
    for grp in range(4):
        for which in range(2):
            x_recv(which, grp).wait_send()


def move_out(*refs):
    for i in range(5):
        refs[5 + i][...] = refs[i][...]


def per_device(attn_inputs, residual, logits, expert_ids, keep_mask, cotangent, up_weight, down_weight):
    vmem = pl.BlockSpec(memory_space=pltpu.VMEM)
    dma = pltpu.SemaphoreType.DMA
    outs = pl.pallas_call(
        kernel,
        out_shape=(
            jax.ShapeDtypeStruct((3, WIN, WIN, C), BF16),
            jax.ShapeDtypeStruct((WIN, WIN, C), BF16),
            jax.ShapeDtypeStruct((2, C, HID), F32),
            jax.ShapeDtypeStruct((2, C, HID), F32),
            jax.ShapeDtypeStruct((WIN * WIN, 1, EXPERTS), F32),
        ),
        in_specs=[vmem] * 8,
        out_specs=(vmem,) * 5,
        scratch_shapes=[
            pltpu.VMEM((2, 3, HALF, C), BF16),
            pltpu.VMEM((224, C), BF16),
            pltpu.VMEM((224, C), BF16),
            pltpu.VMEM((224, 3 * HALF), BF16),
            pltpu.VMEM((2, HALF, C), BF16),
            pltpu.VMEM((80, C), BF16),
            pltpu.VMEM((80, C), BF16),
            pltpu.VMEM((3, TOK, C), BF16),
            pltpu.VMEM((224, C), BF16),
            pltpu.VMEM((224, C), BF16),
            pltpu.VMEM((TOK, C), BF16),
            pltpu.VMEM((TOK, C), BF16),
            pltpu.VMEM((TOK, EXPERTS), F32),
            pltpu.VMEM((TOK, 2), I32),
            pltpu.VMEM((TOK, 2), I32),
            pltpu.VMEM((TOK, 128), F32),
            pltpu.VMEM((TOK, C), BF16),
            pltpu.VMEM((HEADS, TOK, TOK), F32),
            pltpu.VMEM((TOK, TOK), BF16),
            pltpu.VMEM((TOK, TOK), F32),
            pltpu.VMEM((2, 2, HID, C), BF16),
            pltpu.VMEM((NYC, 2, 48, C), BF16),
            pltpu.VMEM((NYC, 2, 48, C), BF16),
            pltpu.VMEM((4, 2, 2, 48, C), BF16),
            pltpu.VMEM((NX, 4, 2, 48, C), BF16),
            pltpu.VMEM((RING, 2, 2, C, HID), BF16),
            pltpu.VMEM((RING, 384, 2 * HID), BF16),
            pltpu.VMEM((RING, 384, 1), F32),
            pltpu.VMEM((NX, 4, 64, C), F32),
            pltpu.VMEM((12, 64, C), BF16),
            pltpu.VMEM((12, 64, C), BF16),
            pltpu.VMEM((NYC, 2, 32, C), BF16),
            pltpu.VMEM((NYC, 2, 32, C), BF16),
            pltpu.VMEM((RING, 2, 2, HID, C), F32),
            pltpu.VMEM((2, 4, 2, 2, HID, C), BF16),
            pltpu.VMEM((2, 4, 2, 2, HID, C), BF16),
            dma((NYC,)), dma((NYC,)),
            dma((3, 4)), dma((3, 4)),
            dma((2, 4, 2, 2)), dma((2, 4, 2, 2)),
            dma((12,)), dma((12,)),
            dma((NYC,)), dma((NYC,)),
            dma((2, 4, 2, 2)), dma((2, 4, 2, 2)),
            dma((3,)), dma((3,)),
            dma((4,)), dma((4,)),
        ],
        compiler_params=pltpu.CompilerParams(
            collective_id=0, has_side_effects=True, vmem_limit_bytes=56 * 1024 * 1024
        ),
    )(
        attn_inputs[:, 0], residual[0], logits.reshape(WIN * WIN, 1, EXPERTS),
        jnp.swapaxes(expert_ids[0], 1, 2), jnp.swapaxes(keep_mask[0], 1, 2), cotangent[0],
        up_weight, down_weight,
    )
    outs = pl.pallas_call(
        move_out,
        out_shape=tuple(jax.ShapeDtypeStruct(o.shape, o.dtype) for o in outs),
        in_specs=[vmem] * 5,
        out_specs=(vmem,) * 5,
    )(*outs)
    attn_grad, res_grad, up_grad, down_grad, logit_grad = outs
    return (
        attn_grad[:, None], res_grad[None], up_grad, down_grad,
        logit_grad.reshape(1, WIN, WIN, EXPERTS),
    )


def solution(mesh):
    in_specs = (
        P(None, "expert", "space", None, None),
        P("expert", "space", None, None),
        P("expert", "space", None, None),
        P("expert", "space", None, None),
        P("expert", "space", None, None),
        P("expert", "space", None, None),
        P("expert", None, "space"),
        P("expert", None, "space"),
    )
    out_specs = (
        P(None, "expert", "space", None, None),
        P("expert", "space", None, None),
        P("expert", None, "space"),
        P("expert", None, "space"),
        P("expert", "space", None, None),
    )
    return jax.shard_map(
        per_device, mesh=mesh, in_specs=in_specs, out_specs=out_specs, check_vma=False
    )
```

```python
import jax
import jax.numpy as jnp
from jax import lax
from jax.experimental import pallas as pl
from jax.experimental.pallas import tpu as pltpu
from jax.sharding import PartitionSpec as P

WIN = 12
PADW = 16
TOK = WIN * PADW
HALF = TOK // 2
C = 512
HEADS = 16
EXPERTS = 32
CAP = 12
NE = 16
NX = 4
NZ = 4
RING = 8
NYC = 8
HID = 128
NORM_EPS = 1e-06
SCORE_MASK = -100.0
NO_KEY = -1e30
GELU_C = 0.7978845608028654
GELU_A = 0.044715
F32 = jnp.float32
BF16 = jnp.bfloat16
I32 = jnp.int32


def iota(shape, dim):
    return lax.broadcasted_iota(I32, shape, dim)


def dot(a, b):
    return lax.dot_general(a, b, (((1,), (0,)), ((), ())), preferred_element_type=F32)


def dot_nt(a, b):
    return lax.dot_general(a, b, (((1,), (1,)), ((), ())), preferred_element_type=F32)


def dot_tn(a, b):
    return lax.dot_general(a, b, (((0,), (0,)), ((), ())), preferred_element_type=F32)


def ge(a, n):
    return (a >= n).astype(I32)


def ones_where(cond):
    return jnp.where(cond, 1.0, 0.0).astype(BF16)


def split_tail(x):
    total = x[48:49] + x[49:50]
    high = total.astype(BF16).astype(F32)
    low = total - high
    row = iota((16, C), 0)
    tail = jnp.where(row == 0, high, jnp.where(row == 1, low, 0.0))
    return jnp.concatenate([x[:48], tail], axis=0).astype(BF16)


def kernel(
    attn_hbm, resid_hbm, logit_ref, ids_ref, keep_ref, cot_hbm, up_ref, down_ref,
    attn_out, res_out, up_out, down_out, logit_out,
    qw, qsend, qrecv, pack_s, gw, gsend, grecv, agrad, asend, arecv,
    resid_s, cot_s, lg_s, ids_s, keep_s, cols, stage, probs, perm_s, bias_s,
    attn_ref, resid_ref, cot_ref, in_sem, gswap, send_rows, recv_rows, rows_two, rows_all, w_all, pg_s, dots_s, part, xs, xr,
    ret_send, ret_recv, grads, zsend, zrecv,
    d_ss, d_rs, g_ss, g_rs, w_ss, w_rs, x_ss, x_rs, r_ss, r_rs, z_ss, z_rs, h_ss, h_rs, s_ss, s_rs,
):
    me_e = lax.axis_index("expert")
    me_s = lax.axis_index("space")
    mx = me_s // NZ
    mz = me_s % NZ
    zhi = me_e // 8
    x1 = mx + 1 - 2 * (mx % 2)
    x3 = NX - 1 - mx
    x2 = NX - 1 - x1
    me_yc = me_e % NYC
    mine = mx * (NX - 1 - mx) // 2
    other = 1 - mine
    zr = zhi * NZ + mz
    dev_x1 = x1 * NZ + mz
    dev_x3 = x3 * NZ + mz
    ring = []
    for step in (1, RING - 1):
        to = (zr + step) % RING
        ring.append(((to // NZ) * NYC + me_yc, mx * NZ + to % NZ))
    after = (me_s + 1) % (NX * NZ)
    before = (me_s + NX * NZ - 1) % (NX * NZ)

    def remote(src, dst, ss, rs, e, s):
        return pltpu.make_async_remote_copy(
            src_ref=src, dst_ref=dst, send_sem=ss, recv_sem=rs,
            device_id={"expert": e, "space": s}, device_id_type=pl.DeviceIdType.MESH,
        )

    fetched = [
        pltpu.make_async_copy(src, dst, in_sem.at[i])
        for i, (src, dst) in enumerate(
            ((attn_hbm, attn_ref), (resid_hbm, resid_ref), (cot_hbm, cot_ref))
        )
    ]
    for cp in fetched:
        cp.start()
    barrier = pltpu.get_barrier_semaphore()

    def greet(e, s):
        pl.semaphore_signal(
            barrier, inc=1, device_id={"expert": e, "space": s}, device_id_type=pl.DeviceIdType.MESH
        )

    @pl.loop(1, NYC)
    def _(i):
        greet(zhi * NYC + (me_yc + i) % NYC, me_s)

    for e, s in ring:
        greet(e, s)
    for s in (dev_x1, dev_x3, after, before):
        greet(me_e, s)

    pl.semaphore_wait(barrier, NYC - 1 + 6)

    def weight_copy(way, step, m, j):
        chunk = (zr - step) % RING if way == 0 else (zr + step) % RING
        src = (up_ref, down_ref)[m].at[mine] if step == 0 and j == 0 else w_all.at[chunk, m, j]
        return remote(
            src, w_all.at[chunk, m, j], w_ss.at[way, step, m, j], w_rs.at[way, step, m, j], *ring[way]
        )

    def weight_arrived(way, step, m, j):
        chunk = (zr - 1 - step) % RING if way == 0 else (zr + 1 + step) % RING
        remote(
            w_all.at[chunk, m, j], w_all.at[chunk, m, j], w_ss.at[way, step, m, j],
            w_rs.at[way, step, m, j], *ring[way],
        ).wait_recv()

    pieces = [(m, j) for j in range(2) for m in range(2)]
    sent_w = []

    def start_weight(way, step, m, j):
        cp = weight_copy(way, step, m, j)
        cp.start()
        sent_w.append(cp)

    def forward_weights(step, j):
        for m in range(2):
            for way in range(2):
                weight_arrived(way, step - 1, m, j)
                if step < 3 or m == way:
                    start_weight(way, step, m, j)

    swap_w = [
        remote((up_ref, down_ref)[m].at[other], w_all.at[zr, m, 1], s_ss.at[m], s_rs.at[m], me_e, dev_x1)
        for m in range(2)
    ]
    for m in range(2):
        swap_w[m].start()
        for way in range(2):
            start_weight(way, 0, m, 0)

    half_rows = WIN // 2
    qw[...] = jnp.zeros((2, 3, HALF, C), BF16)
    resid_s[...] = jnp.zeros((TOK, C), BF16)
    cot_s[...] = jnp.zeros((TOK, C), BF16)
    lg_s[...] = jnp.zeros((TOK, EXPERTS), F32)
    ids_s[...] = jnp.full((TOK, 2), -1, I32)
    keep_s[...] = jnp.zeros((TOK, 2), I32)
    for cp in fetched:
        cp.wait()
    for r in range(WIN):
        at = pl.ds(r * PADW, WIN)
        resid_s[at, :] = resid_ref[r]
        cot_s[at, :] = cot_ref[r]
        lg_s[at, :] = logit_ref[pl.ds(r * WIN, WIN), 0, :]
        for ref, to in ((ids_ref, ids_s), (keep_ref, keep_s)):
            for k in range(2):
                line = ref[r, pl.ds(k, 1), :]
                to[at, pl.ds(k, 1)] = jnp.sum(
                    jnp.where(iota((WIN, WIN), 0) == iota((WIN, WIN), 1), line, 0), axis=1, keepdims=True
                )
    for r in range(half_rows):
        for k in range(3):
            qw[1, k, pl.ds(r * PADW, WIN), :] = attn_ref[k, r]
            qw[0, k, pl.ds(r * PADW, WIN), :] = attn_ref[k, half_rows + r]

    def packing(count, dense):
        wide, narrow = count * HALF, dense
        i = iota((narrow, wide), 0)
        o = iota((narrow, wide), 1)
        keep_row = (o % PADW < WIN) & ((o // PADW) * WIN + o % PADW == i)
        return ones_where(keep_row)

    pack_s[...] = packing(3, 224)
    qsend[...] = dot(pack_s[...], qw[1].reshape(3 * HALF, C)).astype(BF16)
    halo_q = remote(qsend, qrecv, h_ss.at[0], h_rs.at[0], me_e, before)
    halo_q.start()

    resid = resid_s[...].astype(F32)
    rms = jnp.sqrt(jnp.mean(resid * resid, axis=-1, keepdims=True) + NORM_EPS)
    nf = resid / rms
    normed = nf.astype(BF16)
    cot = cot_s[...].astype(F32)
    lg = lg_s[...]
    ids = ids_s[...]
    keep = keep_s[...].astype(F32)
    id1, id2 = ids[:, 0:1], ids[:, 1:2]
    keep1, keep2 = keep[:, 0:1], keep[:, 1:2]
    expert = iota((TOK, EXPERTS), 1)
    oh1 = jnp.where(expert == id1, 1.0, 0.0)
    oh2 = jnp.where(expert == id2, 1.0, 0.0)
    l1 = jnp.sum(jnp.where(expert == id1, lg, 0.0), axis=-1, keepdims=True)
    l2 = jnp.sum(jnp.where(expert == id2, lg, 0.0), axis=-1, keepdims=True)
    lm = jnp.maximum(l1, l2)
    e1, e2 = jnp.exp(l1 - lm), jnp.exp(l2 - lm)
    gate1, gate2 = e1 / (e1 + e2), e2 / (e1 + e2)
    scaled1 = (gate1 * keep1 * cot).astype(BF16)
    scaled2 = (gate2 * keep2 * cot).astype(BF16)
    square_r, square_c = iota((TOK, TOK), 0), iota((TOK, TOK), 1)
    counts = dot(ones_where(square_c < square_r), (oh1 + oh2).astype(BF16))
    slot1 = jnp.sum(oh1 * counts, axis=-1, keepdims=True).astype(I32)
    slot2 = jnp.sum(oh2 * counts, axis=-1, keepdims=True).astype(I32)
    q1 = id1 * CAP + slot1
    q2 = id2 * CAP + slot2
    q1_row = jnp.sum(jnp.where(square_r == square_c, q1, 0), axis=0, keepdims=True)
    q2_row = jnp.sum(jnp.where(square_r == square_c, q2, 0), axis=0, keepdims=True)
    lane = iota((TOK, 128), 1)
    column = jnp.zeros((TOK, 128), F32)
    for i, v in enumerate((gate1, gate2, rms, keep1, keep2)):
        column = jnp.where(lane == i, v, column)
    cols[...] = column

    row = iota((TOK, 1), 0)
    src4 = ge(row, 48) + ge(row, 96) + ge(row, 144)
    rem = row - 48 * src4
    second = ge(rem, 24)

    @pl.loop(0, 2)
    def _(h):
        for p in range(2):
            q = (p * NYC + h * 4 + src4) * 24 + rem - 24 * second
            m1 = q == q1_row
            m2 = q == q2_row
            pn = ones_where((m1 | m2) & (second == 0))
            ps1 = ones_where(m1 & (second == 1))
            ps2 = ones_where(m2 & (second == 1))
            built = dot(pn, normed) + dot(ps1, scaled1) + dot(ps2, scaled2)
            send_rows[pl.ds(h * 4, 4), p] = built.astype(BF16).reshape(4, 48, C)
        for s in range(4):
            to = h * 4 + s

            @pl.when(to != me_yc)
            def _():
                remote(
                    send_rows.at[to], recv_rows.at[me_yc], d_ss.at[to], d_rs.at[me_yc],
                    zhi * NYC + to, me_s,
                ).start()

    recv_rows[me_yc] = send_rows[me_yc]
    for m in range(2):
        swap_w[m].wait_recv()
        for way in range(2):
            start_weight(way, 0, m, 1)

    b96 = ge(row, 96)
    o2 = row - 96 * b96
    b48 = ge(o2, 48)
    o3 = o2 - 48 * b48
    s12 = ge(o3, 12) + ge(o3, 24) + ge(o3, 36)
    perm_s[...] = ones_where(square_c == s12 * 48 + b48 * 24 + b96 * 12 + (o3 - 12 * s12))

    forward_weights(1, 0)

    @pl.loop(0, 2)
    def _(g):
        for s in range(4):
            frm = g * 4 + s

            @pl.when(frm != me_yc)
            def _():
                remote(
                    send_rows.at[frm], recv_rows.at[frm], d_ss.at[frm], d_rs.at[frm],
                    zhi * NYC + frm, me_s,
                ).wait()

        for p in range(2):
            grp = 2 * p + g
            block = recv_rows[pl.ds(g * 4, 4), p].reshape(TOK, C)
            rows_two[grp] = dot(perm_s[...], block).astype(BF16).reshape(2, 2, 48, C)
            for which, j, dev in ((0, other, dev_x1), (1, mine, dev_x3)):
                remote(
                    rows_two.at[grp, j], rows_all.at[mx, grp], g_ss.at[which, grp],
                    g_rs.at[which, grp], me_e, dev,
                ).start()
            rows_all[mx, grp] = rows_two[grp, mine]

    forward_weights(1, 1)
    w_all[zr, 0, 0] = up_ref[mine]
    w_all[zr, 1, 0] = down_ref[mine]

    pos_r = square_r % PADW
    pos_c = square_c % PADW
    differ = (pos_r >= half_rows) != (pos_c >= half_rows)
    is_last = me_s == NX * NZ - 1
    last_i = jnp.where(is_last, 1, 0)
    half_differ = (ge(square_r, HALF) != ge(square_c, HALF)) & ((square_r * 0 + last_i) == 1)
    bias = jnp.where(differ | half_differ, SCORE_MASK, 0.0)
    bias_s[...] = jnp.where(pos_c >= WIN, NO_KEY, bias)
    inv_sqrt = (C // HEADS) ** (-0.5)
    halo_q.wait_recv()
    qw[1] = dot_tn(pack_s[...], qrecv[...]).astype(BF16).reshape(3, HALF, C)

    head_lane = iota((1, 128), 1)

    def head_mask(h):
        return ones_where((head_lane >= h * 32) & (head_lane < (h + 1) * 32))

    @pl.loop(0, 4)
    def _(lg_i):
        lanes = pl.ds(pl.multiple_of(lg_i * 128, 128), 128)
        q = jnp.concatenate([qw[0, 0, :, lanes], qw[1, 0, :, lanes]], axis=0)
        k = jnp.concatenate([qw[0, 1, :, lanes], qw[1, 1, :, lanes]], axis=0)
        for h in range(4):
            sc = dot_nt(q * head_mask(h), k) * inv_sqrt + bias_s[...]
            ex = jnp.exp(sc - jnp.max(sc, axis=-1, keepdims=True))
            probs[lg_i * 4 + h] = ex / jnp.sum(ex, axis=-1, keepdims=True)

    def x_recv(which, grp):
        frm, dev = ((x1, dev_x1), (x3, dev_x3))[which]
        return remote(
            rows_all.at[frm, grp], rows_all.at[frm, grp], g_ss.at[which, grp], g_rs.at[which, grp],
            me_e, dev,
        )

    fwd_x = []

    def forward_rows(grp):
        x_recv(0, grp).wait_recv()
        cp = remote(
            rows_all.at[x1, grp], rows_all.at[x1, grp], g_ss.at[2, grp], g_rs.at[2, grp], me_e, dev_x3
        )
        cp.start()
        fwd_x.append(cp)

    forward_rows(0)
    forward_rows(2)
    forward_weights(2, 0)
    forward_rows(1)
    forward_rows(3)
    forward_weights(2, 1)
    forward_weights(3, 0)
    forward_weights(3, 1)
    for grp in range(4):
        x_recv(1, grp).wait_recv()
    for cp in fwd_x:
        cp.wait_recv()

    def rows_of(p, a):
        return rows_all[:, pl.ds(2 * p, 2), a].reshape(384, C)

    def slice_of(c, m):
        return jnp.concatenate([w_all[c, m, 0], w_all[c, m, 1]], axis=1)

    def expert_slice(c):
        p = c // NZ
        xn = rows_of(p, 0)
        xsc = rows_of(p, 1)
        pre = dot(xn, slice_of(c, 0))
        sq = pre * pre
        t = jnp.tanh(GELU_C * pre * (1.0 + GELU_A * sq))
        act = (0.5 * pre * (1.0 + t)).astype(BF16)
        slope = 0.5 * (1.0 + t) + 0.5 * GELU_C * pre * (1.0 - t * t) * (1.0 + 3.0 * GELU_A * sq)
        dact = dot(xsc, slice_of(c, 1))
        dots_s[c] = jnp.sum(act.astype(F32) * dact, axis=-1, keepdims=True)
        pg = (dact * slope).astype(BF16)
        pg_s[c] = pg
        grads[c, 0] = dot_tn(pg, xn).reshape(2, HID, C)
        grads[c, 1] = dot_tn(act, xsc).reshape(2, HID, C)

    def row_grads(p):
        pg = jnp.concatenate([pg_s[p * NZ + c] for c in range(NZ)], axis=1)
        up = jnp.concatenate([slice_of(p * NZ + c, 0) for c in range(NZ)], axis=1)
        part[:, pl.ds(2 * p, 2), pl.ds(0, 48), :] = dot_nt(pg, up).reshape(4, 2, 48, C)
        dsum = dots_s[p * NZ]
        for c in range(1, NZ):
            dsum = dsum + dots_s[p * NZ + c]
        hit = iota((48, C), 1) == iota((48, C), 0)
        for b in range(NX):
            for g in range(2):
                lo = (2 * b + g) * 48
                line = jnp.sum(jnp.where(hit, dsum[lo : lo + 48], 0.0), axis=0, keepdims=True)
                part[b, 2 * p + g, pl.ds(48, 16), :] = jnp.where(iota((16, C), 0) == 0, line, 0.0)

    def x_send(n, dev, slot, sem):
        return remote(xs.at[n], xr.at[slot], x_ss.at[n], x_rs.at[sem], me_e, dev)

    sent_z = []

    def start_sum(way, step, m, j, add):
        to = (zr + 4 - step) % RING if way == 0 else (zr + 4 + step) % RING
        value = grads[to, m, j]
        if add:
            cp = remote(
                zsend.at[way, step - 1, m, j], zrecv.at[way, step - 1, m, j],
                z_ss.at[way, step - 1, m, j], z_rs.at[way, step - 1, m, j], *ring[way],
            )
            cp.wait_recv()
            value = value + zrecv[way, step - 1, m, j].astype(F32)
        zsend[way, step, m, j] = value.astype(BF16)
        cp = remote(
            zsend.at[way, step, m, j], zrecv.at[way, step, m, j], z_ss.at[way, step, m, j],
            z_rs.at[way, step, m, j], *ring[way],
        )
        cp.start()
        sent_z.append(cp)

    def x_got(slot):
        return remote(xs.at[slot], xr.at[slot], x_ss.at[slot], x_rs.at[slot], me_e, dev_x1)

    sums = []
    def send_sum(slot, dev, value):
        xs[slot] = split_tail(value)
        sums.append(x_send(slot, dev, slot, slot))
        sums[-1].start()

    def away(n):
        return (zr + n + RING) % RING

    expert_slice(away(3))
    for j in (1, 0):
        start_sum(0, 1, 1, j, False)
    expert_slice(away(-3))
    for j in (1, 0):
        start_sum(1, 1, 0, j, False)
    for n in (0, 1, -1, 2, -2):
        expert_slice(away(n))
    row_grads(zhi)
    for g in range(2):
        send_sum(2 * zhi + g, dev_x3, part[x2, 2 * zhi + g])
    for g in range(2):
        send_sum(4 + 2 * zhi + g, dev_x3, part[x3, 2 * zhi + g])
    for way in range(2):
        for j in range(2):
            weight_arrived(way, 3, way, j)
    expert_slice(away(4))
    turn = [(m, j) for j in (1, 0) for m in range(2)]
    for m, j in turn:
        start_sum(m, 0, m, j, False)
    far = 1 - zhi
    row_grads(far)
    for g in range(2):
        send_sum(2 * far + g, dev_x3, part[x2, 2 * far + g])
    for g in range(2):
        send_sum(4 + 2 * far + g, dev_x3, part[x3, 2 * far + g])

    def relay(grp):
        x_got(grp).wait_recv()
        send_sum(8 + grp, dev_x1, part[x1, grp] + xr[grp].astype(F32))

    for g in range(2):
        relay(2 * zhi + g)
    for m, j in turn:
        start_sum(m, 1, m, j, True)
    for g in range(2):
        relay(2 * far + g)
    for j in (1, 0):
        for way in range(2):
            start_sum(way, 2, 1 - way, j, True)

    ro = iota((128, 128), 0)
    rs = ge(ro, 32) + ge(ro, 64) + ge(ro, 96)
    rq = ro - 32 * rs
    rj = ge(rq, 12)
    half_of = jnp.where(rj == mine, 0, 64)
    want = half_of + rs * 12 + rq - 12 * rj
    want = jnp.where(rq < 24, want, jnp.where(rq < 26, rq + 24, jnp.where(rq < 28, rq + 86, -1)))
    back = ones_where(iota((128, 128), 1) == want)
    for g in range(2):
        for p in range(2):
            grp = 2 * p + g
            x_got(4 + grp).wait_recv()
            x_got(8 + grp).wait_recv()
            total = split_tail(part[mx, grp] + xr[4 + grp].astype(F32))
            both = jnp.concatenate([total, xr[8 + grp]], axis=0)
            ret_send[pl.ds(g * 4, 4), p] = dot(back, both).astype(BF16).reshape(4, 32, C)
        for s in range(4):
            to = g * 4 + s

            @pl.when(to != me_yc)
            def _():
                remote(
                    ret_send.at[to], ret_recv.at[me_yc], r_ss.at[to], r_rs.at[me_yc],
                    zhi * NYC + to, me_s,
                ).start()

    ret_recv[me_yc] = ret_send[me_yc]
    for j in (1, 0):
        for way in range(2):
            start_sum(way, 2, way, j, True)

    @pl.loop(0, NYC)
    def _(frm):
        @pl.when(frm != me_yc)
        def _():
            remote(
                ret_send.at[frm], ret_recv.at[frm], r_ss.at[frm], r_rs.at[frm],
                zhi * NYC + frm, me_s,
            ).wait()

    for j in (1, 0):
        for way in range(2):
            start_sum(way, 3, 1 - way, j, True)

    returned = ret_recv[...].reshape(NE * 32, C)
    ids = ids_s[...]
    id1, id2 = ids[:, 0:1], ids[:, 1:2]
    expert = iota((TOK, EXPERTS), 1)
    hot1, hot2 = expert == id1, expert == id2
    oh1, oh2 = jnp.where(hot1, 1.0, 0.0), jnp.where(hot2, 1.0, 0.0)
    counts = dot(ones_where(square_c < square_r), (oh1 + oh2).astype(BF16))
    slot1 = jnp.sum(oh1 * counts, axis=-1, keepdims=True).astype(I32)
    slot2 = jnp.sum(oh2 * counts, axis=-1, keepdims=True).astype(I32)
    q1 = id1 * CAP + slot1
    q2 = id2 * CAP + slot2
    col = iota((TOK, NE * 32), 1)
    block_of = lax.shift_right_arithmetic(col, 5)
    pos = col - 32 * block_of
    dev = lax.shift_right_arithmetic(block_of, 1) + NYC * (block_of % 2)
    at = dev * 24 + pos
    pick = ones_where(((at == q1) | (at == q2)) & (pos < 24))
    norm_grad = dot(pick, returned)
    rms = cols[:, 2:3]
    resid = resid_s[...].astype(F32)
    nf = resid / rms
    inner = jnp.mean(norm_grad * nf, axis=-1, keepdims=True)
    cot = cot_s[...].astype(F32)
    res_grad = (cot + (norm_grad - nf * inner) / rms).astype(BF16)
    stage[...] = res_grad
    pack_one = packing(1, 80)
    gsend[...] = dot(pack_one, stage[pl.ds(0, HALF), :]).astype(BF16)
    halo_g = remote(gsend, grecv, h_ss.at[1], h_rs.at[1], me_e, before)
    halo_g.start()
    gw[0] = stage[pl.ds(HALF, HALF), :]
    for r in range(WIN):
        res_out[r] = stage[pl.ds(r * PADW, WIN), :]

    gate1, gate2 = cols[:, 0:1], cols[:, 1:2]
    keep1, keep2 = cols[:, 3:4], cols[:, 4:5]
    narrow = returned[:, :128]

    def gathered(idk, slotk):
        half = lax.shift_right_arithmetic(idk, 1)
        line = jnp.where(idk - 2 * half == mine, 24, 26)
        pickk = ones_where((dev == half) & ((pos == line) | (pos == line + 1)))
        found = dot(pickk, narrow)
        spot = (me_e % 4) * 12 + slotk
        return jnp.sum(jnp.where(iota((TOK, 128), 1) == spot, found, 0.0), axis=-1, keepdims=True)

    d1 = gathered(id1, slot1)
    d2 = gathered(id2, slot2)
    part1 = gate2 * d1 - gate1 * d2
    share = jnp.sum(oh1 * keep1 + oh2 * keep2, axis=0, keepdims=True) / (2.0 * WIN * WIN)
    lg = lg_s[...]
    lex = jnp.exp(lg - jnp.max(lg, axis=-1, keepdims=True))
    rp = lex / jnp.sum(lex, axis=-1, keepdims=True)
    share_mean = jnp.sum(rp * share, axis=-1, keepdims=True)
    lg_s[...] = (oh1 - oh2) * part1 + EXPERTS * rp * (share - share_mean)
    for r in range(WIN):
        logit_out[pl.ds(r * WIN, WIN), 0, :] = lg_s[pl.ds(r * PADW, WIN), :]

    for j in (1, 0):
        for way in range(2):
            start_sum(way, 3, way, j, True)

    halo_g.wait_recv()
    gw[1] = dot_tn(pack_one, grecv[...]).astype(BF16)

    @pl.loop(0, 4)
    def _(lg_i):
        lanes = pl.ds(pl.multiple_of(lg_i * 128, 128), 128)
        q = jnp.concatenate([qw[0, 0, :, lanes], qw[1, 0, :, lanes]], axis=0)
        k = jnp.concatenate([qw[0, 1, :, lanes], qw[1, 1, :, lanes]], axis=0)
        v = jnp.concatenate([qw[0, 2, :, lanes], qw[1, 2, :, lanes]], axis=0)
        gs = jnp.concatenate([gw[0, :, lanes], gw[1, :, lanes]], axis=0)
        dq = jnp.zeros((TOK, 128), F32)
        dk = jnp.zeros((TOK, 128), F32)
        dv = jnp.zeros((TOK, 128), F32)
        for h in range(4):
            hm = head_mask(h)
            gm = gs * hm
            pr = probs[lg_i * 4 + h]
            wt = pr.astype(BF16)
            pgrad = dot_nt(gm, v)
            delta = jnp.sum(wt.astype(F32) * pgrad, axis=-1, keepdims=True)
            sg = (pr * (pgrad - delta)).astype(BF16)
            dq = dq + dot(sg, k * hm)
            dk = dk + dot_tn(sg, q * hm)
            dv = dv + dot_tn(wt, gm)
        agrad[0, :, lanes] = (dq * inv_sqrt).astype(BF16)
        agrad[1, :, lanes] = (dk * inv_sqrt).astype(BF16)
        agrad[2, :, lanes] = dv.astype(BF16)

    asend[...] = dot(pack_s[...], agrad[:, pl.ds(HALF, HALF), :].reshape(3 * HALF, C)).astype(BF16)
    halo_a = remote(asend, arecv, h_ss.at[2], h_rs.at[2], me_e, after)
    halo_a.start()
    for r in range(half_rows):
        for k in range(3):
            attn_out[k, half_rows + r] = agrad[k, pl.ds(r * PADW, WIN), :]

    swap_g = []
    for j in (1, 0):
        for m, out in ((0, up_out), (1, down_out)):
            value = grads[zr, m, j]
            for way in range(2):
                remote(
                    zsend.at[way, 3, m, j], zrecv.at[way, 3, m, j], z_ss.at[way, 3, m, j],
                    z_rs.at[way, 3, m, j], *ring[way],
                ).wait_recv()
                value = value + zrecv[way, 3, m, j].astype(F32)
            if j == 1:
                gswap[0, m] = value.astype(BF16)
                cp = remote(gswap.at[0, m], gswap.at[1, m], s_ss.at[2 + m], s_rs.at[2 + m], me_e, dev_x1)
                cp.start()
                swap_g.append(cp)
            else:
                out[mine] = value.T
    for m, out in ((0, up_out), (1, down_out)):
        swap_g[m].wait_recv()
        out[other] = gswap[1, m].astype(F32).T

    halo_a.wait_recv()
    qw[1] = dot_tn(pack_s[...], arecv[...]).astype(BF16).reshape(3, HALF, C)
    for r in range(half_rows):
        for k in range(3):
            attn_out[k, r] = qw[1, k, pl.ds(r * PADW, WIN), :]

    for cp in (*sent_w, *swap_w, *fwd_x, *sums, *sent_z, *swap_g, halo_q, halo_g, halo_a):
        cp.wait_send()
    for grp in range(4):
        for which in range(2):
            x_recv(which, grp).wait_send()


def move_out(*refs):
    held, sems = refs[10:15], refs[15]
    reads = [pltpu.make_async_copy(refs[i], held[i], sems.at[0, i]) for i in range(5)]
    writes = [pltpu.make_async_copy(held[i], refs[5 + i], sems.at[1, i]) for i in range(5)]
    for cp in reads:
        cp.start()
    for i in range(5):
        reads[i].wait()
        writes[i].start()
    for cp in writes:
        cp.wait()


def per_device(attn_inputs, residual, logits, expert_ids, keep_mask, cotangent, up_weight, down_weight):
    vmem = pl.BlockSpec(memory_space=pltpu.VMEM)
    anywhere = pl.BlockSpec(memory_space=pl.ANY)
    dma = pltpu.SemaphoreType.DMA
    outs = pl.pallas_call(
        kernel,
        out_shape=(
            jax.ShapeDtypeStruct((3, WIN, WIN, C), BF16),
            jax.ShapeDtypeStruct((WIN, WIN, C), BF16),
            jax.ShapeDtypeStruct((2, C, HID), F32),
            jax.ShapeDtypeStruct((2, C, HID), F32),
            jax.ShapeDtypeStruct((WIN * WIN, 1, EXPERTS), F32),
        ),
        in_specs=[anywhere, anywhere, vmem, vmem, vmem, anywhere, vmem, vmem],
        out_specs=(vmem,) * 5,
        scratch_shapes=[
            pltpu.VMEM((2, 3, HALF, C), BF16),
            pltpu.VMEM((224, C), BF16),
            pltpu.VMEM((224, C), BF16),
            pltpu.VMEM((224, 3 * HALF), BF16),
            pltpu.VMEM((2, HALF, C), BF16),
            pltpu.VMEM((80, C), BF16),
            pltpu.VMEM((80, C), BF16),
            pltpu.VMEM((3, TOK, C), BF16),
            pltpu.VMEM((224, C), BF16),
            pltpu.VMEM((224, C), BF16),
            pltpu.VMEM((TOK, C), BF16),
            pltpu.VMEM((TOK, C), BF16),
            pltpu.VMEM((TOK, EXPERTS), F32),
            pltpu.VMEM((TOK, 2), I32),
            pltpu.VMEM((TOK, 2), I32),
            pltpu.VMEM((TOK, 128), F32),
            pltpu.VMEM((TOK, C), BF16),
            pltpu.VMEM((HEADS, TOK, TOK), F32),
            pltpu.VMEM((TOK, TOK), BF16),
            pltpu.VMEM((TOK, TOK), F32),
            pltpu.VMEM((3, WIN, WIN, C), BF16),
            pltpu.VMEM((WIN, WIN, C), BF16),
            pltpu.VMEM((WIN, WIN, C), BF16),
            dma((3,)),
            pltpu.VMEM((2, 2, HID, C), BF16),
            pltpu.VMEM((NYC, 2, 48, C), BF16),
            pltpu.VMEM((NYC, 2, 48, C), BF16),
            pltpu.VMEM((4, 2, 2, 48, C), BF16),
            pltpu.VMEM((NX, 4, 2, 48, C), BF16),
            pltpu.VMEM((RING, 2, 2, C, HID), BF16),
            pltpu.VMEM((RING, 384, 2 * HID), BF16),
            pltpu.VMEM((RING, 384, 1), F32),
            pltpu.VMEM((NX, 4, 64, C), F32),
            pltpu.VMEM((12, 64, C), BF16),
            pltpu.VMEM((12, 64, C), BF16),
            pltpu.VMEM((NYC, 2, 32, C), BF16),
            pltpu.VMEM((NYC, 2, 32, C), BF16),
            pltpu.VMEM((RING, 2, 2, HID, C), F32),
            pltpu.VMEM((2, 4, 2, 2, HID, C), BF16),
            pltpu.VMEM((2, 4, 2, 2, HID, C), BF16),
            dma((NYC,)), dma((NYC,)),
            dma((3, 4)), dma((3, 4)),
            dma((2, 4, 2, 2)), dma((2, 4, 2, 2)),
            dma((12,)), dma((12,)),
            dma((NYC,)), dma((NYC,)),
            dma((2, 4, 2, 2)), dma((2, 4, 2, 2)),
            dma((3,)), dma((3,)),
            dma((4,)), dma((4,)),
        ],
        compiler_params=pltpu.CompilerParams(
            collective_id=0, has_side_effects=True, vmem_limit_bytes=56 * 1024 * 1024
        ),
    )(
        attn_inputs[:, 0], residual[0], logits.reshape(WIN * WIN, 1, EXPERTS),
        jnp.swapaxes(expert_ids[0], 1, 2), jnp.swapaxes(keep_mask[0], 1, 2), cotangent[0],
        up_weight, down_weight,
    )
    outs = pl.pallas_call(
        move_out,
        out_shape=tuple(jax.ShapeDtypeStruct(o.shape, o.dtype) for o in outs),
        in_specs=[anywhere] * 5,
        out_specs=(anywhere,) * 5,
        scratch_shapes=[pltpu.VMEM(o.shape, o.dtype) for o in outs] + [dma((2, 5))],
    )(*outs)
    attn_grad, res_grad, up_grad, down_grad, logit_grad = outs
    return (
        attn_grad[:, None], res_grad[None], up_grad, down_grad,
        logit_grad.reshape(1, WIN, WIN, EXPERTS),
    )


def solution(mesh):
    in_specs = (
        P(None, "expert", "space", None, None),
        P("expert", "space", None, None),
        P("expert", "space", None, None),
        P("expert", "space", None, None),
        P("expert", "space", None, None),
        P("expert", "space", None, None),
        P("expert", None, "space"),
        P("expert", None, "space"),
    )
    out_specs = (
        P(None, "expert", "space", None, None),
        P("expert", "space", None, None),
        P("expert", None, "space"),
        P("expert", None, "space"),
        P("expert", "space", None, None),
    )
    return jax.shard_map(
        per_device, mesh=mesh, in_specs=in_specs, out_specs=out_specs, check_vma=False
    )
```
